32 devices in a mesh: leaf: 32 (over z, y, x, core).
Axes of the slice: x: 2, y: 2, z: 4, core: 2. Of those that a mesh axis runs over, the one named last changes fastest.
Arguments:
- right_sides: bfloat16 [32, 65536], P(None, 'leaf'), may hold values from -6 to 6
- point_order: int32 [32, 2048], P('leaf'), may hold values from 0 to 2047, each once within a row
- leaf_inverse: bfloat16 [65536, 2048], P('leaf'), may hold values from -0.09375 to 0.09375
- basis_in: bfloat16 [65536, 256], P('leaf'), may hold values from -0.125 to 0.125
- basis_out: bfloat16 [8192, 2048], P('leaf'), may hold values from -0.1875 to 0.1875
- leaf_up: bfloat16 [8192, 256], P('leaf'), may hold values from -0.25 to 0.25
- leaf_down: bfloat16 [8192, 256], P('leaf'), may hold values from -0.3125 to 0.3125
- node_up: bfloat16 [8192, 256], P('leaf'), may hold values from -0.25 to 0.25
- node_down: bfloat16 [8192, 256], P('leaf'), may hold values from -0.3125 to 0.3125
- node_cross: bfloat16 [16384, 256], P('leaf'), may hold values from -0.25 to 0.25
- leaf_map: int32 [32], replicated, may hold values from 0 to 31, as said below
Outputs:
- solution: float32 [32, 65536], P(None, 'leaf')
The draws below stay inside these ranges and needn't reach their ends.
Inputs may be any that keep to these rules, and one draw needn't show every extreme that they name: `point_order`: each row is a permutation of the leaf's columns. `leaf_map`: A permutation of the tree positions that keeps every device's leaf inside the device's aligned block of 4 devices.
All inputs are finite; a program needn't handle non-finite values.
Results may differ from the reference program's by a relative error of at most 0.015.
Values may be sent and summed in bfloat16 or wider, within the bound.
No kernel may reach another device: no remote copies, remote signals or barrier semaphores. Data moves between devices by JAX's collectives and lax.ppermute only.
A program may use at most 192 MiB of HBM per device.

```python
import jax
import jax.numpy as jnp
from jax import lax

LEAF = 2048
RANK = 256
RHS = 32
SPREAD = 4
LEAVES = 32
POINTS = 65536
N_LEAF = 32


def draw_leaf_map(key, part):
    groups = LEAVES // SPREAD
    keys = jax.random.split(jax.random.fold_in(key, 7), groups)
    local = jax.vmap(lambda single: jax.random.permutation(single, SPREAD))(keys)
    offsets = (jnp.arange(groups, dtype=jnp.int32) * SPREAD)[:, None]
    return (local.astype(jnp.int32) + offsets).reshape(LEAVES).astype(jnp.int32)


def shard_levels(key, dims, cuts, least, high):
    gain = 1.0
    for dim, parts in cuts:
        heights = jax.random.uniform(jax.random.fold_in(jax.random.fold_in(key, 6), dim), (parts,), jnp.float32, least / len(cuts), high / len(cuts))
        gain = gain * jnp.repeat(jnp.exp(heights), dims[dim] // parts).reshape((-1,) + (1,) * (len(dims) - 1 - dim))
    return gain


def scatter_about(own_key, extent, scale, bound, pieces=(), kind=jnp.bfloat16):
    array = scale * jax.random.normal(own_key, extent, jnp.float32)
    if pieces:
        array = array * shard_levels(own_key, extent, pieces, -0.22, 0.18)
    return jnp.clip(array, -bound, bound).astype(kind)


def setup_inputs(seed: int = 0) -> dict:
    arg_keys = jax.random.split(jax.random.key(seed), 12)
    return {
        "right_sides": scatter_about(arg_keys[0], (RHS, POINTS), 1.0, 6.0, ((1, 32),)),
        "point_order": jax.vmap(lambda own: jax.random.permutation(own, LEAF))(jax.random.split(arg_keys[1], LEAVES)).reshape((LEAVES, LEAF)).astype(jnp.int32),
        "leaf_inverse": scatter_about(arg_keys[2], (POINTS, LEAF), (2 * LEAF) ** -0.5, 0.09375, ((0, 32),)),
        "basis_in": scatter_about(arg_keys[3], (POINTS, RANK), LEAF ** -0.5, 0.125, ((0, 32),)),
        "basis_out": scatter_about(arg_keys[4], (LEAVES * RANK, LEAF), (4 * RANK) ** -0.5, 0.1875, ((0, 32),)),
        "leaf_up": scatter_about(arg_keys[5], (LEAVES * RANK, RANK), (2 * RANK) ** -0.5, 0.25, ((0, 32),)),
        "leaf_down": scatter_about(arg_keys[6], (LEAVES * RANK, RANK), (4 * RANK // 3) ** -0.5, 0.3125, ((0, 32),)),
        "node_up": scatter_about(arg_keys[7], (LEAVES * RANK, RANK), (2 * RANK) ** -0.5, 0.25, ((0, 32),)),
        "node_down": scatter_about(arg_keys[8], (LEAVES * RANK, RANK), (4 * RANK // 3) ** -0.5, 0.3125, ((0, 32),)),
        "node_cross": scatter_about(arg_keys[9], (LEAVES * 2 * RANK, RANK), (2 * RANK) ** -0.5, 0.25, ((0, 32),)),
        "leaf_map": draw_leaf_map(jax.random.fold_in(arg_keys[11], 71), 0),
    }


def reference(right_sides, point_order, leaf_inverse, basis_in, basis_out, leaf_up, leaf_down, node_up, node_down, node_cross, leaf_map):
    members = N_LEAF
    levels = members.bit_length() - 1
    blocks = jnp.transpose(right_sides.reshape(RHS, members, LEAF), (1, 0, 2))
    tree_rhs = jnp.take_along_axis(blocks, point_order[:, None, :], axis=2)
    inverses = leaf_inverse.reshape(members, LEAF, LEAF)
    inward = basis_in.reshape(members, LEAF, RANK)
    outward = basis_out.reshape(members, RANK, LEAF)

    def leaf_terms(items):
        segment, inverse, basis = items
        near = jnp.dot(segment, inverse, preferred_element_type=jnp.float32)
        coarse = jnp.dot(segment, basis, preferred_element_type=jnp.float32).astype(jnp.bfloat16)
        return near, coarse

    near_terms, reduced = lax.map(leaf_terms, (tree_rhs, inverses, inward))
    source = jnp.zeros((members,), jnp.int32).at[leaf_map].set(jnp.arange(members, dtype=jnp.int32))
    current = reduced[source]
    leaf_ups = leaf_up.reshape(members, RANK, RANK).astype(jnp.float32)
    leaf_downs = leaf_down.reshape(members, RANK, RANK).astype(jnp.float32)
    node_ups = node_up.reshape(members, RANK, RANK).astype(jnp.float32)
    node_downs = node_down.reshape(members, RANK, RANK).astype(jnp.float32)
    couplings = node_cross.reshape(members, 2, RANK, RANK).astype(jnp.float32)
    stored = []
    for height in range(1, levels + 1):
        children = members >> (height - 1)
        if height == 1:
            up_maps = leaf_ups
        else:
            owners = (1 << (height - 1)) * jnp.arange(children) + (1 << (height - 2))
            up_maps = node_ups[owners]
        product = jnp.einsum("nab,nbc->nac", current.astype(jnp.float32), up_maps)
        stored.append((current[0::2], current[1::2]))
        current = (product[0::2] + product[1::2]).astype(jnp.bfloat16)
    top_map = node_up.reshape(members, RANK, RANK)[members // 2]
    node_f = jnp.dot(current[0], top_map, preferred_element_type=jnp.float32).astype(jnp.bfloat16)[None]
    for height in range(levels, 0, -1):
        left_g, right_g = stored[height - 1]
        parents = members >> height
        owners = (1 << height) * jnp.arange(parents) + (1 << (height - 1))
        pair = couplings[owners]
        if height == 1:
            down_maps = leaf_downs
        else:
            child_owners = (1 << (height - 1)) * jnp.arange(2 * parents) + (1 << (height - 2))
            down_maps = node_downs[child_owners]
        parent_f = node_f.astype(jnp.float32)
        left_f = jnp.einsum("nab,nbc->nac", right_g.astype(jnp.float32), pair[:, 0]) + jnp.einsum("nab,nbc->nac", parent_f, down_maps[0::2])
        right_f = jnp.einsum("nab,nbc->nac", left_g.astype(jnp.float32), pair[:, 1]) + jnp.einsum("nab,nbc->nac", parent_f, down_maps[1::2])
        node_f = jnp.stack([left_f.astype(jnp.bfloat16), right_f.astype(jnp.bfloat16)], 1).reshape(2 * parents, RHS, RANK)
    leaf_f = node_f[leaf_map]

    def finish(items):
        near, coarse, basis, ordering = items
        answer = near + jnp.dot(coarse, basis, preferred_element_type=jnp.float32)
        return jnp.zeros_like(answer).at[:, ordering].set(answer)

    placed = lax.map(finish, (near_terms, leaf_f, outward, point_order))
    return jnp.transpose(placed, (1, 0, 2)).reshape(RHS, members * LEAF)
```

```python
import functools

import jax
import jax.numpy as jnp
from jax import lax
from jax.experimental import pallas as pl
from jax.experimental.pallas import tpu as pltpu
from jax.sharding import PartitionSpec as P

SPREAD = 4
LANES = 128
BF = jnp.bfloat16
F32 = jnp.float32
VMEM = pl.BlockSpec(memory_space=pltpu.VMEM)
SMEM = pl.BlockSpec(memory_space=pltpu.SMEM)
ANY = pl.BlockSpec(memory_space=pl.ANY)
LIMIT = 32 * 2**20


def mm(a, b):
    return jnp.dot(a, b, preferred_element_type=F32)


def params():
    return pltpu.CompilerParams(vmem_limit_bytes=LIMIT)


def cost(flops, nbytes):
    return pl.CostEstimate(flops=flops, bytes_accessed=nbytes, transcendentals=0)


def swap(block, mask):
    count = lax.axis_size("leaf")
    return lax.ppermute(block, "leaf", [(i, i ^ mask) for i in range(count)])


def gather_columns(table, slots, store):
    rows, columns = table.shape
    tiles = columns // LANES
    for out_tile in range(tiles):
        slot = jnp.broadcast_to(slots(out_tile), (rows, LANES))
        low = slot & (LANES - 1)
        high = slot // LANES
        found = None
        for tile in range(tiles):
            part = jnp.take_along_axis(
                table[:, tile * LANES : (tile + 1) * LANES], low, axis=1
            )
            found = part if found is None else jnp.where(high == tile, part, found)
        store(out_tile, found)


def entry_kernel(rhs_hbm, order_hbm, basis_hbm, tree_ref, red_ref, rhs, order, basis, table, sems):
    copies = [
        pltpu.make_async_copy(rhs_hbm, rhs, sems.at[0]),
        pltpu.make_async_copy(order_hbm, order, sems.at[1]),
        pltpu.make_async_copy(basis_hbm, basis, sems.at[2]),
    ]
    for copy in copies:
        copy.start()
    copies[0].wait()
    table[...] = rhs[...].astype(F32)
    copies[1].wait()

    def store(tile, found):
        tree_ref[:, tile * LANES : (tile + 1) * LANES] = found.astype(BF)

    gather_columns(
        table, lambda tile: order[:, tile * LANES : (tile + 1) * LANES], store
    )
    copies[2].wait()
    red_ref[...] = mm(tree_ref[...], basis[...]).astype(BF)


def entry(right_sides, point_order, basis_in):
    rows, columns = right_sides.shape
    rank = basis_in.shape[1]
    return pl.pallas_call(
        entry_kernel,
        out_shape=(
            jax.ShapeDtypeStruct((rows, columns), BF),
            jax.ShapeDtypeStruct((rows, rank), BF),
        ),
        in_specs=[ANY] * 3,
        out_specs=(VMEM, VMEM),
        scratch_shapes=[
            pltpu.VMEM(right_sides.shape, BF),
            pltpu.VMEM(point_order.shape, jnp.int32),
            pltpu.VMEM(basis_in.shape, BF),
            pltpu.VMEM(right_sides.shape, F32),
            pltpu.SemaphoreType.DMA((3,)),
        ],
        compiler_params=params(),
        cost_estimate=cost(2 * rows * columns * rank, columns * rank * 2),
        name="entry",
    )(right_sides, point_order, basis_in)


def invert_kernel(order_ref, inv_ref):
    slot = order_ref[...]
    columns = slot.shape[1]
    tiles = columns // LANES
    low = slot & (LANES - 1)
    high = slot // LANES
    here = lax.broadcasted_iota(jnp.int32, (tiles, columns), 1)
    mask = lax.broadcasted_iota(jnp.int32, (tiles, columns), 0) == high
    left = jnp.concatenate(
        [
            jnp.where(mask, (here // LANES).astype(F32), 0.0),
            jnp.where(mask, (here & (LANES - 1)).astype(F32), 0.0),
        ],
        0,
    ).astype(BF)
    right = (lax.broadcasted_iota(jnp.int32, (LANES, columns), 0) == low).astype(F32).astype(BF)
    both = lax.dot_general(left, right, (((1,), (1,)), ((), ())), preferred_element_type=F32)
    inv_ref[...] = (both[:tiles] * LANES + both[tiles:]).astype(jnp.int32)


def invert(point_order):
    columns = point_order.shape[1]
    return pl.pallas_call(
        invert_kernel,
        out_shape=jax.ShapeDtypeStruct((columns // LANES, LANES), jnp.int32),
        in_specs=[VMEM],
        out_specs=VMEM,
        compiler_params=params(),
        cost_estimate=cost(2 * 32 * columns * LANES, columns * 4),
        name="invert",
    )(point_order)


def near_kernel(tree_ref, inverse_ref, near_ref):
    near_ref[...] = mm(tree_ref[...], inverse_ref[...])


def near_strip(tree, leaf_inverse, strip, strips):
    rows, columns = tree.shape
    width = columns // strips
    half = width // 2
    return pl.pallas_call(
        near_kernel,
        grid=(2,),
        out_shape=jax.ShapeDtypeStruct((rows, width), F32),
        in_specs=[
            pl.BlockSpec((rows, columns), lambda i: (0, 0)),
            pl.BlockSpec((columns, half), lambda i: (0, 2 * strip + i)),
        ],
        out_specs=pl.BlockSpec((rows, half), lambda i: (0, i)),
        compiler_params=params(),
        cost_estimate=cost(2 * rows * columns * width, columns * width * 2),
        name="near",
    )(tree, leaf_inverse)


def rise_kernel(pick, red0, red1, red2, red3, up0, up1, up2, up3, lvl_ref, g0_ref, g1_ref, near_ref, far_ref, table):
    rank = red0.shape[1]
    for m, red in enumerate((red0, red1, red2, red3)):
        table[m] = red[...]
    ups = (up0, up1, up2, up3)
    odd = pick[4] == 1
    sums = []
    for m in range(4):
        leaf = table[pick[m]]
        g0_ref[m] = leaf
        sums.append(mm(leaf, ups[m][:rank, :]))
    own = (sums[0] + sums[1]).astype(BF)
    other = (sums[2] + sums[3]).astype(BF)
    g1_ref[0] = own
    g1_ref[1] = other
    own_map = jnp.where(odd, up0[rank:, :], up1[rank:, :])
    other_map = jnp.where(odd, up2[rank:, :], up3[rank:, :])
    rows = red0.shape[0]
    g2 = (mm(own, own_map) + mm(other, other_map)).astype(BF)
    h2 = mm(g2, up2[rank:, :]).astype(BF)
    near_ref[:rows] = g2
    near_ref[rows:] = h2
    far_ref[:rows] = h2
    far_ref[rows:] = mm(h2, lvl_ref[:rank, :]).astype(BF)


def rise(pick, reds, ups, level_maps):
    rows, rank = reds[0].shape
    return pl.pallas_call(
        rise_kernel,
        out_shape=(
            jax.ShapeDtypeStruct((SPREAD, rows, rank), BF),
            jax.ShapeDtypeStruct((2, rows, rank), BF),
            jax.ShapeDtypeStruct((2 * rows, rank), BF),
            jax.ShapeDtypeStruct((2 * rows, rank), BF),
        ),
        in_specs=[SMEM] + [VMEM] * 9,
        out_specs=(VMEM,) * 4,
        scratch_shapes=[pltpu.VMEM((SPREAD, rows, rank), BF)],
        compiler_params=params(),
        cost_estimate=cost(2 * 8 * rows * rank * rank, 8 * rank * rank * 2),
        name="rise",
    )(pick, *reds, *ups, level_maps)


def pair_kernel(chain, *refs):
    mine, near, far, both, maps = refs[:5]
    following = refs[5 : 5 + chain]
    outs = refs[5 + chain :]
    rows = mine.shape[0] // 2
    rank = mine.shape[1]
    grown = (mine[rows:].astype(F32) + near[rows:].astype(F32)).astype(BF)
    outs[0][...] = (far[:rows].astype(F32) + both[:rows].astype(F32)).astype(BF)
    higher = mm(grown, maps[:rank, :]) + far[rows:].astype(F32) + both[rows:].astype(F32)
    higher = higher.astype(BF)
    if chain == 0:
        outs[1][...] = higher
        return
    sent = mm(higher, following[0][:rank, :]).astype(BF)
    outs[1][:rows] = higher
    outs[1][rows:] = sent
    if chain == 2:
        outs[2][:rows] = sent
        outs[2][rows:] = mm(sent, following[1][:rank, :]).astype(BF)


def pair(mine, near, far, both, maps, following):
    double, rank = mine.shape
    rows = double // 2
    single = jax.ShapeDtypeStruct((rows, rank), BF)
    twofold = jax.ShapeDtypeStruct((double, rank), BF)
    chain = len(following)
    shapes = {0: (single, single), 1: (single, twofold), 2: (single, twofold, twofold)}[chain]
    return pl.pallas_call(
        functools.partial(pair_kernel, chain),
        out_shape=shapes,
        in_specs=[VMEM] * (5 + chain),
        out_specs=(VMEM,) * len(shapes),
        compiler_params=params(),
        cost_estimate=cost(6 * rows * rank * rank, 6 * rank * rank),
        name="pair",
    )(mine, near, far, both, maps, *following)


def fall_kernel(count, *refs):
    top = refs[0]
    siblings = refs[1 : 1 + count]
    maps = refs[1 + count : 1 + 2 * count]
    block_down = refs[1 + 2 * count]
    out = refs[2 + 2 * count]
    rank = top.shape[1]
    value = mm(top[...], maps[count - 1][:rank, :]).astype(BF)
    for k in range(count - 1, -1, -1):
        down = block_down[...] if k == 0 else maps[k - 1][rank : 2 * rank, :]
        cross = maps[k][maps[k].shape[0] - rank :, :]
        value = (mm(siblings[k][...], cross) + mm(value, down)).astype(BF)
    out[...] = value


def fall(top, siblings, maps, block_down):
    count = len(maps)
    rows, rank = top.shape
    return pl.pallas_call(
        functools.partial(fall_kernel, count),
        out_shape=jax.ShapeDtypeStruct((rows, rank), BF),
        in_specs=[VMEM] * (2 + 2 * count),
        out_specs=VMEM,
        compiler_params=params(),
        cost_estimate=cost(12 * rows * rank * rank, 12 * rank * rank),
        name="fall",
    )(top, *siblings, *maps, block_down)


def local_kernel(pick, g0_ref, g1_ref, dn0, dn1, dn2, dn3, r1_ref, r0_ref, e1_ref, e0_ref, b2, b1, sems):
    rank = r0_ref.shape[0]
    packs = (dn0, dn1, dn2, dn3)

    def fetch(mask, row, dst, sem):
        start = pl.multiple_of(row, rank)
        for m in range(4):

            @pl.when(mask == m)
            def _():
                pltpu.make_async_copy(packs[m].at[pl.ds(start, rank), :], dst, sem).start()

    fetch(pick[5], 0, r0_ref, sems.at[0])
    fetch(pick[6], rank, r1_ref, sems.at[1])
    fetch(pick[6], (2 + pick[8]) * rank, b1, sems.at[2])
    fetch(pick[7], (2 + pick[9]) * rank, b2, sems.at[3])
    for i, dst in enumerate((r0_ref, r1_ref, b1, b2)):
        pltpu.make_async_copy(dn0.at[pl.ds(0, rank), :], dst, sems.at[i]).wait()
    e0_ref[...] = mm(g0_ref[pick[10]], b1[...])
    e1_ref[...] = mm(g1_ref[pick[11]], b2[...])


def local(pick, g0, g1, downs):
    _, rows, rank = g0.shape
    square = jax.ShapeDtypeStruct((rank, rank), BF)
    flat = jax.ShapeDtypeStruct((rows, rank), F32)
    return pl.pallas_call(
        local_kernel,
        out_shape=(square, square, flat, flat),
        in_specs=[SMEM, VMEM, VMEM] + [ANY] * 4,
        out_specs=(VMEM,) * 4,
        scratch_shapes=[
            pltpu.VMEM((rank, rank), BF),
            pltpu.VMEM((rank, rank), BF),
            pltpu.SemaphoreType.DMA((4,)),
        ],
        compiler_params=params(),
        cost_estimate=cost(4 * rows * rank * rank, 8 * rank * rank),
        name="local",
    )(pick, g0, g1, *downs)


def final_kernel(strips, f_ref, r1_ref, r0_ref, e1_ref, e0_ref, out_basis, inv_ref, *refs):
    nears = refs[:strips]
    answer, total = refs[strips:]
    f1 = (mm(f_ref[...], r1_ref[...]) + e1_ref[...]).astype(BF)
    f0 = (mm(f1, r0_ref[...]) + e0_ref[...]).astype(BF)
    width = nears[0].shape[1]
    for i in range(strips):
        span = slice(i * width, (i + 1) * width)
        total[:, span] = nears[i][...] + mm(f0, out_basis[:, span])

    def store(tile, found):
        answer[:, tile * LANES : (tile + 1) * LANES] = found

    gather_columns(total, lambda tile: inv_ref[tile : tile + 1, :], store)


def final(f2, r1, r0, e1, e0, basis_out, inverse_order, nears):
    rows, rank = f2.shape
    columns = basis_out.shape[1]
    return pl.pallas_call(
        functools.partial(final_kernel, len(nears)),
        out_shape=jax.ShapeDtypeStruct((rows, columns), F32),
        in_specs=[VMEM] * (7 + len(nears)),
        out_specs=VMEM,
        scratch_shapes=[pltpu.VMEM((rows, columns), F32)],
        compiler_params=params(),
        cost_estimate=cost(2 * rows * rank * columns, rank * columns * 2),
        name="final",
    )(f2, r1, r0, e1, e0, basis_out, inverse_order, *nears)


def body(
    right_sides,
    point_order,
    leaf_inverse,
    basis_in,
    basis_out,
    leaf_up,
    leaf_down,
    node_up,
    node_down,
    node_cross,
    leaf_map,
):
    members = lax.axis_size("leaf")
    levels = members.bit_length() - 1
    cut = SPREAD.bit_length() - 1
    me = lax.axis_index("leaf")
    rank = leaf_up.shape[1]
    offset = me & (SPREAD - 1)

    slots = jnp.arange(SPREAD, dtype=jnp.int32)
    block_map = lax.dynamic_slice(leaf_map, (me - offset,), (SPREAD,)) & (SPREAD - 1)
    wanted = slots ^ offset
    source = jnp.sum(jnp.where(block_map[None, :] == wanted[:, None], slots[None, :], 0), axis=1)
    seat = jnp.sum(jnp.where(slots == offset, block_map, 0))
    mask = seat ^ offset
    node = (seat | 1) ^ offset
    middle = offset ^ (SPREAD // 2)
    pick = jnp.concatenate(
        [
            source ^ offset,
            jnp.stack(
                [
                    offset & 1,
                    mask,
                    node,
                    middle,
                    seat & 1,
                    seat >> 1,
                    mask ^ 1,
                    1 - (mask >> 1),
                ]
            ),
        ]
    ).astype(jnp.int32)

    up_own = jnp.concatenate([leaf_up, node_up], 0)
    up_x = swap(up_own, 2)
    up_core = swap(up_own, 1)
    up_both = swap(up_x, 1)
    down_own = jnp.concatenate([leaf_down, node_down, node_cross], 0)

    level_maps = []
    for level in range(cut + 1, levels + 1):
        parts = [node_up] if level == levels else [node_up, node_down]
        first = jnp.concatenate(parts + [node_cross[:rank]], 0)
        second = jnp.concatenate(parts + [node_cross[rank:]], 0)
        half = 1 << (level - 1)
        arrived = lax.ppermute(
            first, "leaf", [(i + half, i) for i in range(0, members, 2 * half)]
        )
        held = jnp.where(me & half != 0, second, arrived)
        for bit in range(level - 2, cut - 1, -1):
            step = 1 << bit
            arrived = lax.ppermute(
                held, "leaf", [(i, i + step) for i in range(0, members, 2 * step)]
            )
            held = jnp.where(me & step != 0, arrived, held)
        level_maps.append(held)

    tree, reduced = entry(right_sides, point_order, basis_in)
    reds = [reduced] + [swap(reduced, m) for m in range(1, SPREAD)]
    strips = 4
    nears = [near_strip(tree, leaf_inverse, i, strips) for i in range(strips)]
    inverse_order = invert(point_order)

    down_x = swap(down_own, 2)
    down_core = swap(down_own, 1)
    down_both = swap(down_x, 1)

    g0, g1, near, far = rise(pick, reds, [up_own, up_core, up_x, up_both], level_maps[0])
    r1, r0, e1, e0 = local(pick, g0, g1, [down_own, down_core, down_x, down_both])
    rows = right_sides.shape[0]

    siblings = []
    bit = cut
    while bit < levels:
        low = 1 << bit
        near_in = swap(near, low)
        siblings.append(near_in[:rows])
        if bit + 1 < levels:
            far_in = swap(far, 2 * low)
            both_in = swap(far, 3 * low)
            after = bit + 2
            following = [level_maps[i - cut - 1] for i in (after, after + 1) if i < levels]
            results = pair(near, near_in, far_in, both_in, level_maps[bit + 1 - cut - 1], following)
            siblings.append(results[0])
            near = results[1]
            if len(results) == 3:
                far = results[2]
            top = near[:rows]
            bit += 2
        else:
            top = (near[rows:].astype(F32) + near_in[rows:].astype(F32)).astype(BF)
            bit += 1

    block_f = fall(top, siblings, level_maps, down_x[rank : 2 * rank])
    from_x = swap(block_f, 2)
    block_f = jnp.where(offset & 2 != 0, from_x, block_f)
    from_core = swap(block_f, 1)
    block_f = jnp.where(offset & 1 != 0, from_core, block_f)
    return final(block_f, r1, r0, e1, e0, basis_out, inverse_order, nears)


def solution(mesh):
    placed = (
        P(None, "leaf"),
        P("leaf", None),
        P("leaf", None),
        P("leaf", None),
        P("leaf", None),
        P("leaf", None),
        P("leaf", None),
        P("leaf", None),
        P("leaf", None),
        P("leaf", None),
        P(),
    )
    return jax.shard_map(
        body, mesh=mesh, in_specs=placed, out_specs=P(None, "leaf"), check_vma=False
    )
```

```python
import functools

import jax
import jax.numpy as jnp
from jax import lax
from jax.experimental import pallas as pl
from jax.experimental.pallas import tpu as pltpu
from jax.sharding import PartitionSpec as P

SPREAD = 4
LANES = 128
BF = jnp.bfloat16
F32 = jnp.float32
VMEM = pl.BlockSpec(memory_space=pltpu.VMEM)
SMEM = pl.BlockSpec(memory_space=pltpu.SMEM)
ANY = pl.BlockSpec(memory_space=pl.ANY)
LIMIT = 32 * 2**20


def mm(a, b):
    return jnp.dot(a, b, preferred_element_type=F32)


def params():
    return pltpu.CompilerParams(vmem_limit_bytes=LIMIT)


def cost(flops, nbytes):
    return pl.CostEstimate(flops=flops, bytes_accessed=nbytes, transcendentals=0)


def swap(block, mask):
    count = lax.axis_size("leaf")
    return lax.ppermute(block, "leaf", [(i, i ^ mask) for i in range(count)])


def gather_columns(table, slots, store):
    rows, columns = table.shape
    tiles = columns // LANES
    for out_tile in range(tiles):
        slot = jnp.broadcast_to(slots(out_tile), (rows, LANES))
        low = slot & (LANES - 1)
        high = slot // LANES
        found = None
        for tile in range(tiles):
            part = jnp.take_along_axis(
                table[:, tile * LANES : (tile + 1) * LANES], low, axis=1
            )
            found = part if found is None else jnp.where(high == tile, part, found)
        store(out_tile, found)


def start_kernel(rhs_hbm, order_hbm, basis_hbm, map_hbm, leaf_down, node_up, node_down, node_cross,
                 pick, tree_ref, red_ref, down_ref, low_ref, high_ref, toplow_ref, tophigh_ref,
                 rhs, order, basis, table, seats, sems):
    rank = red_ref.shape[1]
    first = [
        pltpu.make_async_copy(rhs_hbm, rhs, sems.at[0]),
        pltpu.make_async_copy(order_hbm, order, sems.at[1]),
        pltpu.make_async_copy(map_hbm, seats, sems.at[2]),
        pltpu.make_async_copy(basis_hbm, basis, sems.at[3]),
    ]
    cross_low = node_cross.at[pl.ds(0, rank), :]
    cross_high = node_cross.at[pl.ds(rank, rank), :]
    packs = [
        (down_ref, (leaf_down, node_down, cross_low, cross_high)),
        (low_ref, (node_up, node_down, cross_low)),
        (high_ref, (node_up, node_down, cross_high)),
        (toplow_ref, (node_up, cross_low)),
        (tophigh_ref, (node_up, cross_high)),
    ]
    rest = []
    for dst, parts in packs:
        for i, part in enumerate(parts):
            rest.append(
                pltpu.make_async_copy(
                    part, dst.at[pl.ds(i * rank, rank), :], sems.at[4 + len(rest)]
                )
            )
    for copy in first + rest:
        copy.start()
    first[0].wait()
    table[...] = rhs[...].astype(F32)
    first[1].wait()

    def store(tile, found):
        tree_ref[:, tile * LANES : (tile + 1) * LANES] = found.astype(BF)

    gather_columns(
        table, lambda tile: order[:, tile * LANES : (tile + 1) * LANES], store
    )
    first[2].wait()
    me = lax.axis_index("leaf").astype(jnp.int32)
    offset = me & (SPREAD - 1)
    base = me - offset
    placed = [seats[base + slot] & (SPREAD - 1) for slot in range(SPREAD)]
    seat = placed[0]
    for slot in range(1, SPREAD):
        seat = jnp.where(offset == slot, placed[slot], seat)
    for m in range(SPREAD):
        source = jnp.int32(0)
        for slot in range(1, SPREAD):
            source = jnp.where(placed[slot] == (offset ^ m), slot, source)
        pick[m] = source ^ offset
    mask = seat ^ offset
    pick[4] = offset & 1
    pick[5] = mask
    pick[6] = (seat | 1) ^ offset
    pick[7] = offset ^ (SPREAD // 2)
    pick[8] = seat & 1
    pick[9] = seat // 2
    pick[10] = mask ^ 1
    pick[11] = 1 - mask // 2
    first[3].wait()
    red_ref[...] = mm(tree_ref[...], basis[...]).astype(BF)
    for copy in rest:
        copy.wait()


def start(right_sides, point_order, basis_in, leaf_map, leaf_down, node_up, node_down, node_cross):
    rows, columns = right_sides.shape
    rank = basis_in.shape[1]

    def block(count):
        return jax.ShapeDtypeStruct((count * rank, rank), BF)

    return pl.pallas_call(
        start_kernel,
        out_shape=(
            jax.ShapeDtypeStruct((12,), jnp.int32),
            jax.ShapeDtypeStruct((rows, columns), BF),
            jax.ShapeDtypeStruct((rows, rank), BF),
            block(4),
            block(3),
            block(3),
            block(2),
            block(2),
        ),
        in_specs=[ANY] * 8,
        out_specs=(SMEM,) + (VMEM,) * 7,
        scratch_shapes=[
            pltpu.VMEM(right_sides.shape, BF),
            pltpu.VMEM(point_order.shape, jnp.int32),
            pltpu.VMEM(basis_in.shape, BF),
            pltpu.VMEM(right_sides.shape, F32),
            pltpu.SMEM(leaf_map.shape, jnp.int32),
            pltpu.SemaphoreType.DMA((18,)),
        ],
        compiler_params=params(),
        cost_estimate=cost(2 * rows * columns * rank, columns * rank * 2),
        name="start",
    )(right_sides, point_order, basis_in, leaf_map, leaf_down, node_up, node_down, node_cross)


def invert_kernel(order_ref, inv_ref):
    slot = order_ref[...]
    columns = slot.shape[1]
    tiles = columns // LANES
    low = slot & (LANES - 1)
    high = slot // LANES
    here = lax.broadcasted_iota(jnp.int32, (tiles, columns), 1)
    mask = lax.broadcasted_iota(jnp.int32, (tiles, columns), 0) == high
    left = jnp.concatenate(
        [
            jnp.where(mask, (here // LANES).astype(F32), 0.0),
            jnp.where(mask, (here & (LANES - 1)).astype(F32), 0.0),
        ],
        0,
    ).astype(BF)
    right = (lax.broadcasted_iota(jnp.int32, (LANES, columns), 0) == low).astype(F32).astype(BF)
    both = lax.dot_general(left, right, (((1,), (1,)), ((), ())), preferred_element_type=F32)
    inv_ref[...] = (both[:tiles] * LANES + both[tiles:]).astype(jnp.int32)


def invert(point_order):
    columns = point_order.shape[1]
    return pl.pallas_call(
        invert_kernel,
        out_shape=jax.ShapeDtypeStruct((columns // LANES, LANES), jnp.int32),
        in_specs=[VMEM],
        out_specs=VMEM,
        compiler_params=params(),
        cost_estimate=cost(2 * 32 * columns * LANES, columns * 4),
        name="invert",
    )(point_order)


def near_kernel(tree_ref, inverse_ref, after, near_ref):
    near_ref[...] = mm(tree_ref[...], inverse_ref[...])


def near_strip(tree, leaf_inverse, strip, strips, after):
    rows, columns = tree.shape
    width = columns // strips
    half = width // 2
    return pl.pallas_call(
        near_kernel,
        grid=(2,),
        out_shape=jax.ShapeDtypeStruct((rows, width), F32),
        in_specs=[
            pl.BlockSpec((rows, columns), lambda i: (0, 0)),
            pl.BlockSpec((columns, half), lambda i: (0, 2 * strip + i)),
            ANY,
        ],
        out_specs=pl.BlockSpec((rows, half), lambda i: (0, i)),
        compiler_params=params(),
        cost_estimate=cost(2 * rows * columns * width, columns * width * 2),
        name="near",
    )(tree, leaf_inverse, after)


def leaf_kernel(pick, red0, red1, red2, red3, up_ref, g0_ref, out_ref, table):
    for m, red in enumerate((red0, red1, red2, red3)):
        table[m] = red[...]
    for m in range(SPREAD):
        g0_ref[m] = table[pick[m]]
    out_ref[...] = mm(g0_ref[0], up_ref[...])


def leaf_rise(pick, reds, leaf_up):
    rows, rank = reds[0].shape
    return pl.pallas_call(
        leaf_kernel,
        out_shape=(
            jax.ShapeDtypeStruct((SPREAD, rows, rank), BF),
            jax.ShapeDtypeStruct((rows, rank), F32),
        ),
        in_specs=[SMEM] + [VMEM] * 5,
        out_specs=(VMEM,) * 2,
        scratch_shapes=[pltpu.VMEM((SPREAD, rows, rank), BF)],
        compiler_params=params(),
        cost_estimate=cost(2 * rows * rank * rank, rank * rank * 2),
        name="leaf_rise",
    )(pick, *reds, leaf_up)


def node_kernel(pick, mine, other, up_own, up_other, out_ref):
    rows = mine.shape[0]
    odd = pick[4] == 1
    g1 = (mine[...] + other[...]).astype(BF)
    out_ref[:rows] = g1
    node_map = jnp.where(odd, up_own[...], up_other[...])
    out_ref[rows:] = mm(g1, node_map).astype(BF)


def node_rise(pick, mine, other, up_own, up_other):
    rows, rank = mine.shape
    return pl.pallas_call(
        node_kernel,
        out_shape=jax.ShapeDtypeStruct((2 * rows, rank), BF),
        in_specs=[SMEM] + [VMEM] * 4,
        out_specs=VMEM,
        compiler_params=params(),
        cost_estimate=cost(2 * rows * rank * rank, rank * rank * 2),
        name="node_rise",
    )(pick, mine, other, up_own, up_other)


def block_kernel(mine, other, up_ref, level_ref, after, g1_ref, near_ref, far_ref):
    rows = mine.shape[0] // 2
    rank = mine.shape[1]
    g1_ref[0] = mine[:rows]
    g1_ref[1] = other[:rows]
    g2 = (mine[rows:].astype(F32) + other[rows:].astype(F32)).astype(BF)
    h2 = mm(g2, up_ref[...]).astype(BF)
    near_ref[:rows] = g2
    near_ref[rows:] = h2
    far_ref[:rows] = h2
    far_ref[rows:] = mm(h2, level_ref[:rank, :]).astype(BF)


def block_rise(mine, other, block_up, level_maps, after):
    double, rank = mine.shape
    rows = double // 2
    return pl.pallas_call(
        block_kernel,
        out_shape=(
            jax.ShapeDtypeStruct((2, rows, rank), BF),
            jax.ShapeDtypeStruct((double, rank), BF),
            jax.ShapeDtypeStruct((double, rank), BF),
        ),
        in_specs=[VMEM] * 4 + [ANY],
        out_specs=(VMEM,) * 3,
        compiler_params=params(),
        cost_estimate=cost(4 * rows * rank * rank, 2 * rank * rank * 2),
        name="block_rise",
    )(mine, other, block_up, level_maps, after)


def pair_kernel(chain, *refs):
    mine, near, far, both, maps = refs[:5]
    following = refs[5 : 5 + chain]
    outs = refs[6 + chain :]
    rows = mine.shape[0] // 2
    rank = mine.shape[1]
    grown = (mine[rows:].astype(F32) + near[rows:].astype(F32)).astype(BF)
    outs[0][...] = (far[:rows].astype(F32) + both[:rows].astype(F32)).astype(BF)
    higher = mm(grown, maps[:rank, :]) + far[rows:].astype(F32) + both[rows:].astype(F32)
    higher = higher.astype(BF)
    if chain == 0:
        outs[1][...] = higher
        return
    sent = mm(higher, following[0][:rank, :]).astype(BF)
    outs[1][:rows] = higher
    outs[1][rows:] = sent
    if chain == 2:
        outs[2][:rows] = sent
        outs[2][rows:] = mm(sent, following[1][:rank, :]).astype(BF)


def pair(mine, near, far, both, maps, following, after):
    double, rank = mine.shape
    rows = double // 2
    single = jax.ShapeDtypeStruct((rows, rank), BF)
    twofold = jax.ShapeDtypeStruct((double, rank), BF)
    chain = len(following)
    shapes = {0: (single, single), 1: (single, twofold), 2: (single, twofold, twofold)}[chain]
    return pl.pallas_call(
        functools.partial(pair_kernel, chain),
        out_shape=shapes,
        in_specs=[VMEM] * (5 + chain) + [ANY],
        out_specs=(VMEM,) * len(shapes),
        compiler_params=params(),
        cost_estimate=cost(6 * rows * rank * rank, 6 * rank * rank),
        name="pair",
    )(mine, near, far, both, maps, *following, after)


def fall_kernel(count, *refs):
    top = refs[0]
    siblings = refs[1 : 1 + count]
    maps = refs[1 + count : 1 + 2 * count]
    cut_maps, out = refs[1 + 2 * count], refs[3 + 2 * count]
    rank = top.shape[1]
    value = mm(top[...], maps[count - 1][:rank, :]).astype(BF)
    for k in range(count - 1, -1, -1):
        down = cut_maps if k == 0 else maps[k - 1]
        cross = maps[k][maps[k].shape[0] - rank :, :]
        value = (mm(siblings[k][...], cross) + mm(value, down[rank : 2 * rank, :])).astype(BF)
    out[...] = value


def fall(top, siblings, maps, cut_maps, after):
    count = len(maps)
    rows, rank = top.shape
    return pl.pallas_call(
        functools.partial(fall_kernel, count),
        out_shape=jax.ShapeDtypeStruct((rows, rank), BF),
        in_specs=[VMEM] * (2 + 2 * count) + [ANY],
        out_specs=VMEM,
        compiler_params=params(),
        cost_estimate=cost(12 * rows * rank * rank, 12 * rank * rank),
        name="fall",
    )(top, *siblings, *maps, cut_maps, after)


def step_kernel(flag, mine, other, sibling, maps, down_pack, after, out):
    rank = mine.shape[1]
    value = jnp.where(flag[0] != 0, other[...], mine[...])
    cross = maps[2 * rank :, :]
    out[...] = (mm(sibling[...], cross) + mm(value, down_pack[rank : 2 * rank, :])).astype(BF)


def step_down(flag, mine, other, sibling, maps, down_pack, after):
    rows, rank = mine.shape
    return pl.pallas_call(
        step_kernel,
        out_shape=jax.ShapeDtypeStruct((rows, rank), BF),
        in_specs=[SMEM] + [VMEM] * 5 + [ANY],
        out_specs=VMEM,
        compiler_params=params(),
        cost_estimate=cost(4 * rows * rank * rank, 4 * rank * rank),
        name="step_down",
    )(flag, mine, other, sibling, maps, down_pack, after)


def local_kernel(pick, g0_ref, g1_ref, dn0, dn1, dn2, dn3, r1_ref, r0_ref, e1_ref, e0_ref, b2, b1, sems):
    rank = r0_ref.shape[0]
    packs = (dn0, dn1, dn2, dn3)

    def fetch(mask, row, dst, sem):
        start = pl.multiple_of(row, rank)
        for m in range(4):

            @pl.when(mask == m)
            def _():
                pltpu.make_async_copy(packs[m].at[pl.ds(start, rank), :], dst, sem).start()

    fetch(pick[5], 0, r0_ref, sems.at[0])
    fetch(pick[6], rank, r1_ref, sems.at[1])
    fetch(pick[6], (2 + pick[8]) * rank, b1, sems.at[2])
    fetch(pick[7], (2 + pick[9]) * rank, b2, sems.at[3])
    for i, dst in enumerate((r0_ref, r1_ref, b1, b2)):
        pltpu.make_async_copy(dn0.at[pl.ds(0, rank), :], dst, sems.at[i]).wait()
    e0_ref[...] = mm(g0_ref[pick[10]], b1[...])
    e1_ref[...] = mm(g1_ref[pick[11]], b2[...])


def local(pick, g0, g1, downs):
    _, rows, rank = g0.shape
    square = jax.ShapeDtypeStruct((rank, rank), BF)
    flat = jax.ShapeDtypeStruct((rows, rank), F32)
    return pl.pallas_call(
        local_kernel,
        out_shape=(square, square, flat, flat),
        in_specs=[SMEM, VMEM, VMEM] + [ANY] * 4,
        out_specs=(VMEM,) * 4,
        scratch_shapes=[
            pltpu.VMEM((rank, rank), BF),
            pltpu.VMEM((rank, rank), BF),
            pltpu.SemaphoreType.DMA((4,)),
        ],
        compiler_params=params(),
        cost_estimate=cost(4 * rows * rank * rank, 8 * rank * rank),
        name="local",
    )(pick, g0, g1, *downs)


def final_kernel(strips, pick, f_own, f_core, r1_ref, r0_ref, e1_ref, e0_ref, out_basis, inv_ref, *refs):
    nears = refs[:strips]
    answer, total = refs[strips:]
    f2 = jnp.where(pick[4] == 1, f_core[...], f_own[...])
    f1 = (mm(f2, r1_ref[...]) + e1_ref[...]).astype(BF)
    f0 = (mm(f1, r0_ref[...]) + e0_ref[...]).astype(BF)
    width = nears[0].shape[1]
    for i in range(strips):
        span = slice(i * width, (i + 1) * width)
        total[:, span] = nears[i][...] + mm(f0, out_basis[:, span])

    def store(tile, found):
        answer[:, tile * LANES : (tile + 1) * LANES] = found

    gather_columns(total, lambda tile: inv_ref[tile : tile + 1, :], store)


def final(pick, f2, f2_core, r1, r0, e1, e0, basis_out, inverse_order, nears):
    rows, rank = f2.shape
    columns = basis_out.shape[1]
    return pl.pallas_call(
        functools.partial(final_kernel, len(nears)),
        out_shape=jax.ShapeDtypeStruct((rows, columns), F32),
        in_specs=[SMEM] + [VMEM] * (8 + len(nears)),
        out_specs=VMEM,
        scratch_shapes=[pltpu.VMEM((rows, columns), F32)],
        compiler_params=params(),
        cost_estimate=cost(2 * rows * rank * columns, rank * columns * 2),
        name="final",
    )(pick, f2, f2_core, r1, r0, e1, e0, basis_out, inverse_order, *nears)


def body(
    right_sides,
    point_order,
    leaf_inverse,
    basis_in,
    basis_out,
    leaf_up,
    leaf_down,
    node_up,
    node_down,
    node_cross,
    leaf_map,
):
    members = lax.axis_size("leaf")
    levels = members.bit_length() - 1
    cut = SPREAD.bit_length() - 1
    me = lax.axis_index("leaf")
    rows = right_sides.shape[0]
    offset = me & (SPREAD - 1)

    pick, tree, reduced, down_own, low, high, top_low, top_high = start(
        right_sides, point_order, basis_in, leaf_map, leaf_down, node_up, node_down, node_cross
    )
    reds = [reduced] + [swap(reduced, m) for m in range(1, SPREAD)]
    up_core = swap(node_up, 1)
    half = SPREAD // 2
    block_up = lax.ppermute(
        node_up, "leaf", [(i + half, i) for i in range(0, members, SPREAD)]
    )

    level_maps = []
    for level in range(cut + 1, levels + 1):
        first, second = (top_low, top_high) if level == levels else (low, high)
        span = 1 << (level - 1)
        arrived = lax.ppermute(
            first, "leaf", [(i + span, i) for i in range(0, members, 2 * span)]
        )
        held = jnp.where(me & span != 0, second, arrived)
        for bit in range(level - 2, cut, -1):
            step = 1 << bit
            arrived = lax.ppermute(
                held, "leaf", [(i, i + step) for i in range(0, members, 2 * step)]
            )
            held = jnp.where(me & step != 0, arrived, held)
        level_maps.append(held)

    inverse_order = invert(point_order)
    down_x = swap(down_own, 2)
    down_core = swap(down_own, 1)
    down_both = swap(down_x, 1)

    g0, product = leaf_rise(pick, reds, leaf_up)
    node_pay = node_rise(pick, product, swap(product, 1), node_up, up_core)
    node_in = swap(node_pay, 2)
    near0 = near_strip(tree, leaf_inverse, 0, 2, node_pay)
    g1, near, far = block_rise(node_pay, node_in, block_up, level_maps[0], near0)

    siblings = []
    bit = cut
    after = near0
    while bit < levels:
        step = 1 << bit
        near_in = swap(near, step)
        siblings.append(near_in[:rows])
        if bit + 1 < levels:
            far_in = swap(far, 2 * step)
            both_in = swap(far, 3 * step)
            if bit == cut:
                near1 = near_strip(tree, leaf_inverse, 1, 2, near)
                after = near1
            following = [level_maps[i - cut - 1] for i in (bit + 2, bit + 3) if i < levels]
            results = pair(near, near_in, far_in, both_in, level_maps[bit - cut], following, after)
            siblings.append(results[0])
            near = results[1]
            if len(results) == 3:
                far = results[2]
            top = near[:rows]
            bit += 2
        else:
            top = (near[rows:].astype(F32) + near_in[rows:].astype(F32)).astype(BF)
            bit += 1

    r1, r0, e1, e0 = local(pick, g0, g1, [down_own, down_core, down_x, down_both])
    cut_f = fall(top, siblings[1:], level_maps[1:], level_maps[0], e0)
    flag = (me >> cut & 1).astype(jnp.int32)[None]
    block_f = step_down(flag, cut_f, swap(cut_f, SPREAD), siblings[0], level_maps[0], down_x, inverse_order)
    from_x = swap(block_f, 2)
    block_f = jnp.where(offset & 2 != 0, from_x, block_f)
    return final(
        pick, block_f, swap(block_f, 1), r1, r0, e1, e0, basis_out, inverse_order, [near0, near1]
    )


def solution(mesh):
    placed = (
        P(None, "leaf"),
        P("leaf", None),
        P("leaf", None),
        P("leaf", None),
        P("leaf", None),
        P("leaf", None),
        P("leaf", None),
        P("leaf", None),
        P("leaf", None),
        P("leaf", None),
        P(),
    )
    return jax.shard_map(
        body, mesh=mesh, in_specs=placed, out_specs=P(None, "leaf"), check_vma=False
    )
```

```python
import functools

import jax
import jax.numpy as jnp
from jax import lax
from jax.experimental import pallas as pl
from jax.experimental.pallas import tpu as pltpu
from jax.sharding import PartitionSpec as P

SPREAD = 4
LANES = 128
BF = jnp.bfloat16
F32 = jnp.float32
VMEM = pl.BlockSpec(memory_space=pltpu.VMEM)
SMEM = pl.BlockSpec(memory_space=pltpu.SMEM)
ANY = pl.BlockSpec(memory_space=pl.ANY)
HBM = pl.BlockSpec(memory_space=pltpu.HBM)
LIMIT = 32 * 2**20


def mm(a, b):
    return jnp.dot(a, b, preferred_element_type=F32)


def params():
    return pltpu.CompilerParams(vmem_limit_bytes=LIMIT)


def cost(flops, nbytes):
    return pl.CostEstimate(flops=flops, bytes_accessed=nbytes, transcendentals=0)


def swap(block, mask):
    count = lax.axis_size("leaf")
    return lax.ppermute(block, "leaf", [(i, i ^ mask) for i in range(count)])


def bit_of_device(bit):
    return (lax.axis_index("leaf").astype(jnp.int32) & (1 << bit)) != 0


def gather_columns(table, slots, store):
    rows, columns = table.shape
    tiles = columns // LANES
    for out_tile in range(tiles):
        slot = jnp.broadcast_to(slots(out_tile), (rows, LANES))
        low = slot & (LANES - 1)
        high = slot // LANES
        found = None
        for tile in range(tiles):
            part = jnp.take_along_axis(
                table[:, tile * LANES : (tile + 1) * LANES], low, axis=1
            )
            found = part if found is None else jnp.where(high == tile, part, found)
        store(out_tile, found)


def start_kernel(rhs_hbm, order_hbm, basis_hbm, map_hbm, pick, tree_ref, red_ref,
                 rhs, order, basis, table, seats, sems):
    copies = [
        pltpu.make_async_copy(rhs_hbm, rhs, sems.at[0]),
        pltpu.make_async_copy(order_hbm, order, sems.at[1]),
        pltpu.make_async_copy(map_hbm, seats, sems.at[2]),
        pltpu.make_async_copy(basis_hbm, basis, sems.at[3]),
    ]
    for copy in copies:
        copy.start()
    copies[2].wait()
    me = lax.axis_index("leaf").astype(jnp.int32)
    offset = me & (SPREAD - 1)
    base = me - offset
    placed = [seats[base + slot] & (SPREAD - 1) for slot in range(SPREAD)]
    seat = placed[0]
    for slot in range(1, SPREAD):
        seat = jnp.where(offset == slot, placed[slot], seat)
    for m in range(SPREAD):
        source = jnp.int32(0)
        for slot in range(1, SPREAD):
            source = jnp.where(placed[slot] == (offset ^ m), slot, source)
        pick[m] = source ^ offset
    pick[SPREAD] = seat ^ offset
    copies[0].wait()
    table[...] = rhs[...].astype(F32)
    copies[1].wait()

    def store(tile, found):
        tree_ref[:, tile * LANES : (tile + 1) * LANES] = found.astype(BF)

    gather_columns(
        table, lambda tile: order[:, tile * LANES : (tile + 1) * LANES], store
    )
    copies[3].wait()
    red_ref[...] = mm(tree_ref[...], basis[...]).astype(BF)


def start(right_sides, point_order, basis_in, leaf_map):
    rows, columns = right_sides.shape
    rank = basis_in.shape[1]
    return pl.pallas_call(
        start_kernel,
        out_shape=(
            jax.ShapeDtypeStruct((SPREAD + 1,), jnp.int32),
            jax.ShapeDtypeStruct((rows, columns), BF),
            jax.ShapeDtypeStruct((rows, rank), BF),
        ),
        in_specs=[HBM] * 4,
        out_specs=(SMEM, VMEM, VMEM),
        scratch_shapes=[
            pltpu.VMEM(right_sides.shape, BF),
            pltpu.VMEM(point_order.shape, jnp.int32),
            pltpu.VMEM(basis_in.shape, BF),
            pltpu.VMEM(right_sides.shape, F32),
            pltpu.SMEM(leaf_map.shape, jnp.int32),
            pltpu.SemaphoreType.DMA((4,)),
        ],
        compiler_params=params(),
        cost_estimate=cost(2 * rows * columns * rank, columns * rank * 2),
        name="start",
    )(right_sides, point_order, basis_in, leaf_map)


def pack_kernel(node_up, node_down, node_cross, after, low_ref, high_ref, fulllow_ref,
                fullhigh_ref, toplow_ref, tophigh_ref, sems):
    rank = node_up.shape[1]
    cross_low = node_cross.at[pl.ds(0, rank), :]
    cross_high = node_cross.at[pl.ds(rank, rank), :]
    packs = [
        (low_ref, (node_down, cross_low)),
        (high_ref, (node_down, cross_high)),
        (fulllow_ref, (node_up, node_down, cross_low)),
        (fullhigh_ref, (node_up, node_down, cross_high)),
        (toplow_ref, (node_up, cross_low)),
        (tophigh_ref, (node_up, cross_high)),
    ]
    copies = []
    for dst, parts in packs:
        for i, part in enumerate(parts):
            copies.append(
                pltpu.make_async_copy(
                    part, dst.at[pl.ds(i * rank, rank), :], sems.at[len(copies)]
                )
            )
    for copy in copies:
        copy.start()
    for copy in copies:
        copy.wait()


def pack(node_up, node_down, node_cross, after):
    rank = node_up.shape[1]
    sizes = (2, 2, 3, 3, 2, 2)
    return pl.pallas_call(
        pack_kernel,
        out_shape=tuple(jax.ShapeDtypeStruct((n * rank, rank), BF) for n in sizes),
        in_specs=[HBM] * 3 + [ANY],
        out_specs=(VMEM,) * 6,
        scratch_shapes=[pltpu.SemaphoreType.DMA((sum(sizes),))],
        compiler_params=params(),
        cost_estimate=cost(0, 14 * rank * rank * 2),
        name="pack",
    )(node_up, node_down, node_cross, after)


def invert_kernel(order_hbm, after, inv_ref, order, sem):
    copy = pltpu.make_async_copy(order_hbm, order, sem)
    copy.start()
    copy.wait()
    slot = order[...]
    columns = slot.shape[1]
    tiles = columns // LANES
    low = slot & (LANES - 1)
    high = slot // LANES
    here = lax.broadcasted_iota(jnp.int32, (tiles, columns), 1)
    mask = lax.broadcasted_iota(jnp.int32, (tiles, columns), 0) == high
    left = jnp.concatenate(
        [
            jnp.where(mask, (here // LANES).astype(F32), 0.0),
            jnp.where(mask, (here & (LANES - 1)).astype(F32), 0.0),
        ],
        0,
    ).astype(BF)
    right = (lax.broadcasted_iota(jnp.int32, (LANES, columns), 0) == low).astype(F32).astype(BF)
    both = lax.dot_general(left, right, (((1,), (1,)), ((), ())), preferred_element_type=F32)
    inv_ref[...] = (both[:tiles] * LANES + both[tiles:]).astype(jnp.int32)


def invert(point_order, after):
    columns = point_order.shape[1]
    return pl.pallas_call(
        invert_kernel,
        out_shape=jax.ShapeDtypeStruct((columns // LANES, LANES), jnp.int32),
        in_specs=[HBM, ANY],
        out_specs=VMEM,
        scratch_shapes=[pltpu.VMEM(point_order.shape, jnp.int32), pltpu.SemaphoreType.DMA],
        compiler_params=params(),
        cost_estimate=cost(2 * 32 * columns * LANES, columns * 4),
        name="invert",
    )(point_order, after)


def near_kernel(first, tree_ref, inverse_hbm, after, near_ref, held, sems):
    chunks, _, width = held.shape
    copies = [
        pltpu.make_async_copy(
            inverse_hbm.at[:, pl.ds(first + i * width, width)], held.at[i], sems.at[i]
        )
        for i in range(chunks)
    ]
    for copy in copies:
        copy.start()
    for i, copy in enumerate(copies):
        copy.wait()
        near_ref[:, i * width : (i + 1) * width] = mm(tree_ref[...], held[i])


def near_strip(tree, leaf_inverse, strip, strips, after):
    rows, columns = tree.shape
    width = columns // strips
    chunk = 2 * LANES
    chunks = width // chunk
    return pl.pallas_call(
        functools.partial(near_kernel, strip * width),
        out_shape=jax.ShapeDtypeStruct((rows, width), F32),
        in_specs=[VMEM, HBM, ANY],
        out_specs=VMEM,
        scratch_shapes=[
            pltpu.VMEM((chunks, columns, chunk), BF),
            pltpu.SemaphoreType.DMA((chunks,)),
        ],
        compiler_params=params(),
        cost_estimate=cost(2 * rows * columns * width, columns * width * 2),
        name="near",
    )(tree, leaf_inverse, after)


def leaf_kernel(pick, red0, red1, red2, red3, up_ref, after, g0_ref, out_ref, table):
    for m, red in enumerate((red0, red1, red2, red3)):
        table[m] = red[...]
    for m in range(SPREAD):
        g0_ref[m] = table[pick[m]]
    out_ref[...] = mm(g0_ref[0], up_ref[...])


def leaf_rise(pick, reds, leaf_up, after):
    rows, rank = reds[0].shape
    return pl.pallas_call(
        leaf_kernel,
        out_shape=(
            jax.ShapeDtypeStruct((SPREAD, rows, rank), BF),
            jax.ShapeDtypeStruct((rows, rank), F32),
        ),
        in_specs=[SMEM] + [VMEM] * 5 + [ANY],
        out_specs=(VMEM,) * 2,
        scratch_shapes=[pltpu.VMEM((SPREAD, rows, rank), BF)],
        compiler_params=params(),
        cost_estimate=cost(2 * rows * rank * rank, rank * rank * 2),
        name="leaf_rise",
    )(pick, *reds, leaf_up, after)


def node_kernel(mine, other, up_own, up_other, out_ref):
    rows = mine.shape[0]
    odd = bit_of_device(0)
    g1 = (mine[...] + other[...]).astype(BF)
    out_ref[:rows] = g1
    node_map = jnp.where(odd, up_own[...], up_other[...])
    out_ref[rows:] = mm(g1, node_map).astype(BF)


def node_rise(mine, other, up_own, up_other):
    rows, rank = mine.shape
    return pl.pallas_call(
        node_kernel,
        out_shape=jax.ShapeDtypeStruct((2 * rows, rank), BF),
        in_specs=[VMEM] * 4,
        out_specs=VMEM,
        compiler_params=params(),
        cost_estimate=cost(2 * rows * rank * rank, rank * rank * 2),
        name="node_rise",
    )(mine, other, up_own, up_other)


def block_kernel(mine, other, up_ref, level_own, level_in, after, g1_ref, near_ref, far_ref):
    rows = mine.shape[0] // 2
    rank = mine.shape[1]
    g1_ref[0] = mine[:rows]
    g1_ref[1] = other[:rows]
    g2 = (mine[rows:].astype(F32) + other[rows:].astype(F32)).astype(BF)
    h2 = mm(g2, up_ref[...]).astype(BF)
    near_ref[:rows] = g2
    near_ref[rows:] = h2
    far_ref[:rows] = h2
    level_map = jnp.where(bit_of_device(SPREAD.bit_length() - 1), level_own[...], level_in[...])
    far_ref[rows:] = mm(h2, level_map).astype(BF)


def block_rise(mine, other, block_up, level_own, level_in, after):
    double, rank = mine.shape
    rows = double // 2
    return pl.pallas_call(
        block_kernel,
        out_shape=(
            jax.ShapeDtypeStruct((2, rows, rank), BF),
            jax.ShapeDtypeStruct((double, rank), BF),
            jax.ShapeDtypeStruct((double, rank), BF),
        ),
        in_specs=[VMEM] * 5 + [ANY],
        out_specs=(VMEM,) * 3,
        compiler_params=params(),
        cost_estimate=cost(4 * rows * rank * rank, 2 * rank * rank * 2),
        name="block_rise",
    )(mine, other, block_up, level_own, level_in, after)


def pair_kernel(bit, chain, *refs):
    mine, near, far, both, maps_own, maps_in = refs[:6]
    following = refs[6 : 6 + chain]
    outs = refs[7 + chain :]
    rows = mine.shape[0] // 2
    rank = mine.shape[1]
    grown = (mine[rows:].astype(F32) + near[rows:].astype(F32)).astype(BF)
    outs[0][...] = (far[:rows].astype(F32) + both[:rows].astype(F32)).astype(BF)
    maps = jnp.where(bit_of_device(bit), maps_own[:rank, :], maps_in[:rank, :])
    higher = mm(grown, maps) + far[rows:].astype(F32) + both[rows:].astype(F32)
    higher = higher.astype(BF)
    if chain == 0:
        outs[1][...] = higher
        return
    sent = mm(higher, following[0][:rank, :]).astype(BF)
    outs[1][:rows] = higher
    outs[1][rows:] = sent
    if chain == 2:
        outs[2][:rows] = sent
        outs[2][rows:] = mm(sent, following[1][:rank, :]).astype(BF)


def pair(bit, mine, near, far, both, maps_own, maps_in, following, after):
    double, rank = mine.shape
    rows = double // 2
    single = jax.ShapeDtypeStruct((rows, rank), BF)
    twofold = jax.ShapeDtypeStruct((double, rank), BF)
    chain = len(following)
    shapes = {0: (single, single), 1: (single, twofold), 2: (single, twofold, twofold)}[chain]
    return pl.pallas_call(
        functools.partial(pair_kernel, bit, chain),
        out_shape=shapes,
        in_specs=[VMEM] * (6 + chain) + [ANY],
        out_specs=(VMEM,) * len(shapes),
        compiler_params=params(),
        cost_estimate=cost(6 * rows * rank * rank, 6 * rank * rank),
        name="pair",
    )(mine, near, far, both, maps_own, maps_in, *following, after)


def fall_kernel(count, *refs):
    top = refs[0]
    siblings = refs[1 : 1 + count]
    maps = refs[1 + count : 1 + 2 * count]
    cut_maps, out = refs[1 + 2 * count], refs[3 + 2 * count]
    rank = top.shape[1]
    value = mm(top[...], maps[count - 1][:rank, :]).astype(BF)
    for k in range(count - 1, -1, -1):
        down = cut_maps[:rank, :] if k == 0 else maps[k - 1][rank : 2 * rank, :]
        cross = maps[k][maps[k].shape[0] - rank :, :]
        value = (mm(siblings[k][...], cross) + mm(value, down)).astype(BF)
    out[...] = value


def fall(top, siblings, maps, cut_maps, after):
    count = len(maps)
    rows, rank = top.shape
    return pl.pallas_call(
        functools.partial(fall_kernel, count),
        out_shape=jax.ShapeDtypeStruct((rows, rank), BF),
        in_specs=[VMEM] * (2 + 2 * count) + [ANY],
        out_specs=VMEM,
        compiler_params=params(),
        cost_estimate=cost(12 * rows * rank * rank, 12 * rank * rank),
        name="fall",
    )(top, *siblings, *maps, cut_maps, after)


def step_kernel(bit, mine, other, sibling, maps_own, maps_in, down_pack, after, out):
    rank = mine.shape[1]
    upper = bit_of_device(bit)
    value = jnp.where(upper, other[...], mine[...])
    cross = jnp.where(upper, maps_own[rank:, :], maps_in[rank:, :])
    out[...] = (mm(sibling[...], cross) + mm(value, down_pack[:rank, :])).astype(BF)


def step_down(bit, mine, other, sibling, maps_own, maps_in, down_pack, after):
    rows, rank = mine.shape
    return pl.pallas_call(
        functools.partial(step_kernel, bit),
        out_shape=jax.ShapeDtypeStruct((rows, rank), BF),
        in_specs=[VMEM] * 6 + [ANY],
        out_specs=VMEM,
        compiler_params=params(),
        cost_estimate=cost(4 * rows * rank * rank, 4 * rank * rank),
        name="step_down",
    )(mine, other, sibling, maps_own, maps_in, down_pack, after)


def local_kernel(g0_ref, g1_ref, down_ref, node_own, node_in, block_own, block_in, out_ref):
    rank = down_ref.shape[0]
    odd = bit_of_device(0)
    node = jnp.where(odd, node_own[...], node_in[...])
    cross = jnp.where(odd, block_in[rank:, :], block_own[rank:, :])
    out_ref[:rank] = mm(node[:rank, :], down_ref[...]).astype(BF)
    inner = mm(g1_ref[1], cross).astype(BF)
    out_ref[rank:] = (mm(g0_ref[1], node[rank:, :]) + mm(inner, down_ref[...])).astype(BF)


def local(g0, g1, leaf_down, node_own, node_in, block_own, block_in):
    _, rows, rank = g0.shape
    return pl.pallas_call(
        local_kernel,
        out_shape=jax.ShapeDtypeStruct((rank + rows, rank), BF),
        in_specs=[VMEM] * 7,
        out_specs=VMEM,
        compiler_params=params(),
        cost_estimate=cost(2 * (rank + 3 * rows) * rank * rank, 8 * rank * rank),
        name="local",
    )(g0, g1, leaf_down, node_own, node_in, block_own, block_in)


def final_kernel(strips, pick, f_own, f_core, l0, l1, l2, l3, out_basis, inv_ref, *refs):
    nears = refs[:strips]
    answer, total, leaf_f = refs[strips:]
    rank = f_own.shape[1]
    f2 = jnp.where(bit_of_device(0), f_core[...], f_own[...])
    for m, pack_ref in enumerate((l0, l1, l2, l3)):

        @pl.when(pick[SPREAD] == m)
        def _():
            leaf_f[...] = (mm(f2, pack_ref[:rank, :]) + pack_ref[rank:, :].astype(F32)).astype(BF)

    width = nears[0].shape[1]
    for i in range(strips):
        span = slice(i * width, (i + 1) * width)
        total[:, span] = nears[i][...] + mm(leaf_f[...], out_basis[:, span])

    def store(tile, found):
        answer[:, tile * LANES : (tile + 1) * LANES] = found

    gather_columns(total, lambda tile: inv_ref[tile : tile + 1, :], store)


def final(pick, f2, f2_core, locals_, basis_out, inverse_order, nears):
    rows, rank = f2.shape
    columns = basis_out.shape[1]
    return pl.pallas_call(
        functools.partial(final_kernel, len(nears)),
        out_shape=jax.ShapeDtypeStruct((rows, columns), F32),
        in_specs=[SMEM] + [VMEM] * (8 + len(nears)),
        out_specs=VMEM,
        scratch_shapes=[pltpu.VMEM((rows, columns), F32), pltpu.VMEM((rows, rank), BF)],
        compiler_params=params(),
        cost_estimate=cost(2 * rows * rank * columns, rank * columns * 2),
        name="final",
    )(pick, f2, f2_core, *locals_, basis_out, inverse_order, *nears)


def body(
    right_sides,
    point_order,
    leaf_inverse,
    basis_in,
    basis_out,
    leaf_up,
    leaf_down,
    node_up,
    node_down,
    node_cross,
    leaf_map,
):
    members = lax.axis_size("leaf")
    levels = members.bit_length() - 1
    cut = SPREAD.bit_length() - 1
    me = lax.axis_index("leaf")
    rows = right_sides.shape[0]
    offset = me & (SPREAD - 1)

    def to_left(block, bit):
        step = 1 << bit
        return lax.ppermute(block, "leaf", [(i + step, i) for i in range(0, members, 2 * step)])

    def to_right(block, bit, every):
        step = 1 << bit
        pairs = [(i, i + step) for i in range(0, members, every) if i & step == 0]
        return lax.ppermute(block, "leaf", pairs)

    block_up = to_left(node_up, 1)
    group_up = to_left(node_up, 2)
    node_up_in = swap(node_up, 1)

    pick, tree, reduced = start(right_sides, point_order, basis_in, leaf_map)
    reds = [reduced] + [swap(reduced, m) for m in range(1, SPREAD)]
    low, high, full_low, full_high, top_low, top_high = pack(node_up, node_down, node_cross, reduced)

    level_maps = []
    for level in range(cut + 2, levels + 1):
        first, second = (top_low, top_high) if level == levels else (full_low, full_high)
        span = 1 << (level - 1)
        held = jnp.where(me & span != 0, second, to_left(first, level - 1))
        for bit in range(level - 2, cut, -1):
            arrived = to_right(held, bit, 1 << bit)
            held = jnp.where(me & (1 << bit) != 0, arrived, held)
        level_maps.append(held)
    group_in = to_left(low, cut)
    block_in = to_left(low, 1)
    block_held = jnp.where(offset & 2 != 0, high, block_in)
    block_core = to_right(block_held, 0, 2)
    node_in = to_left(low, 0)

    g0, product = leaf_rise(pick, reds, leaf_up, low)
    node_pay = node_rise(product, swap(product, 1), node_up, node_up_in)
    pay_in = swap(node_pay, 2)
    near0 = near_strip(tree, leaf_inverse, 0, 2, node_pay)
    g1, near, far = block_rise(node_pay, pay_in, block_up, node_up, group_up, near0)

    own_local = local(g0, g1, leaf_down, high, node_in, block_held, block_core)
    local_x = swap(own_local, 2)
    locals_ = [own_local, swap(own_local, 1), local_x, swap(local_x, 1)]

    siblings = []
    bit = cut
    after = near0
    while bit < levels:
        step = 1 << bit
        near_in = swap(near, step)
        siblings.append(near_in[:rows])
        if bit + 1 < levels:
            far_in = swap(far, 2 * step)
            both_in = swap(far, 3 * step)
            if bit == cut:
                maps_own, maps_in = node_up, group_up
                near1 = near_strip(tree, leaf_inverse, 1, 2, near)
                after = near1
            else:
                maps_own = maps_in = level_maps[bit - cut - 1]
            following = [level_maps[i - cut - 2] for i in (bit + 2, bit + 3) if i < levels]
            results = pair(bit, near, near_in, far_in, both_in, maps_own, maps_in, following, after)
            siblings.append(results[0])
            near = results[1]
            if len(results) == 3:
                far = results[2]
            top = near[:rows]
            bit += 2
        else:
            top = (near[rows:].astype(F32) + near_in[rows:].astype(F32)).astype(BF)
            bit += 1

    inverse_order = invert(point_order, near1)
    cut_f = fall(top, siblings[1:], level_maps, group_in, inverse_order)
    block_f = step_down(
        cut, cut_f, swap(cut_f, SPREAD), siblings[0], high, group_in, block_held, own_local
    )
    from_x = swap(block_f, 2)
    block_f = jnp.where(offset & 2 != 0, from_x, block_f)
    return final(
        pick, block_f, swap(block_f, 1), locals_, basis_out, inverse_order, [near0, near1]
    )


def solution(mesh):
    placed = (
        P(None, "leaf"),
        P("leaf", None),
        P("leaf", None),
        P("leaf", None),
        P("leaf", None),
        P("leaf", None),
        P("leaf", None),
        P("leaf", None),
        P("leaf", None),
        P("leaf", None),
        P(),
    )
    return jax.shard_map(
        body, mesh=mesh, in_specs=placed, out_specs=P(None, "leaf"), check_vma=False
    )
```

```python
import functools

import jax
import jax.numpy as jnp
from jax import lax
from jax.experimental import pallas as pl
from jax.experimental.pallas import tpu as pltpu
from jax.sharding import PartitionSpec as P

SPREAD = 4
LANES = 128
BF = jnp.bfloat16
F32 = jnp.float32
VMEM = pl.BlockSpec(memory_space=pltpu.VMEM)
SMEM = pl.BlockSpec(memory_space=pltpu.SMEM)
ANY = pl.BlockSpec(memory_space=pl.ANY)
HBM = pl.BlockSpec(memory_space=pltpu.HBM)
LIMIT = 32 * 2**20


def mm(a, b):
    return jnp.dot(a, b, preferred_element_type=F32)


def params():
    return pltpu.CompilerParams(vmem_limit_bytes=LIMIT)


def in_hbm(*arrays):
    return [pltpu.with_memory_space_constraint(array, pltpu.HBM) for array in arrays]


def took(micros):
    return pl.CostEstimate(flops=0, bytes_accessed=int(micros * 3e6), transcendentals=0)


def swap(block, mask):
    count = lax.axis_size("leaf")
    return lax.ppermute(block, "leaf", [(i, i ^ mask) for i in range(count)])


def bit_of_device(bit):
    return (lax.axis_index("leaf").astype(jnp.int32) & (1 << bit)) != 0


def held(bit, own, arrived, begin, size):
    rows = slice(begin, begin + size)
    if own is arrived:
        return own[rows, :]
    return jnp.where(bit_of_device(bit), own[rows, :], arrived[rows, :])


def gather_columns(table, slots, store):
    rows, columns = table.shape
    tiles = columns // LANES
    for out_tile in range(tiles):
        slot = jnp.broadcast_to(slots(out_tile), (rows, LANES))
        low = slot & (LANES - 1)
        high = slot // LANES
        found = None
        for tile in range(tiles):
            part = jnp.take_along_axis(
                table[:, tile * LANES : (tile + 1) * LANES], low, axis=1
            )
            found = part if found is None else jnp.where(high == tile, part, found)
        store(out_tile, found)


def start_kernel(rhs_hbm, order_hbm, basis_hbm, map_hbm, leaf_up, leaf_down, node_up, node_down, node_cross,
                 pick, tree_ref, red_ref, low_ref, high_ref, toplow_ref, tophigh_ref, up_ref, down_ref,
                 rhs, order, basis, table, seats, sems):
    rank = red_ref.shape[1]
    cross_low = node_cross.at[pl.ds(0, rank), :]
    cross_high = node_cross.at[pl.ds(rank, rank), :]
    copies = [
        pltpu.make_async_copy(rhs_hbm, rhs, sems.at[0]),
        pltpu.make_async_copy(order_hbm, order, sems.at[1]),
        pltpu.make_async_copy(map_hbm, seats, sems.at[2]),
        pltpu.make_async_copy(basis_hbm, basis, sems.at[3]),
    ]
    packs = (
        (low_ref, (node_up, node_down, cross_low)),
        (high_ref, (node_up, node_down, cross_high)),
        (toplow_ref, (node_up, cross_low)),
        (tophigh_ref, (node_up, cross_high)),
        (up_ref, (leaf_up,)),
        (down_ref, (leaf_down,)),
    )
    for dst, parts in packs:
        for i, part in enumerate(parts):
            copies.append(
                pltpu.make_async_copy(
                    part, dst.at[pl.ds(i * rank, rank), :], sems.at[len(copies)]
                )
            )
    for copy in copies:
        copy.start()
    copies[2].wait()
    me = lax.axis_index("leaf").astype(jnp.int32)
    offset = me & (SPREAD - 1)
    base = me - offset
    placed = [seats[base + slot] & (SPREAD - 1) for slot in range(SPREAD)]
    seat = placed[0]
    for slot in range(1, SPREAD):
        seat = jnp.where(offset == slot, placed[slot], seat)
    for m in range(SPREAD):
        source = jnp.int32(0)
        for slot in range(1, SPREAD):
            source = jnp.where(placed[slot] == (offset ^ m), slot, source)
        pick[m] = source ^ offset
    pick[SPREAD] = seat ^ offset
    copies[0].wait()
    table[...] = rhs[...].astype(F32)
    copies[1].wait()

    def store(tile, found):
        tree_ref[:, tile * LANES : (tile + 1) * LANES] = found.astype(BF)

    gather_columns(
        table, lambda tile: order[:, tile * LANES : (tile + 1) * LANES], store
    )
    copies[3].wait()
    red_ref[...] = mm(tree_ref[...], basis[...]).astype(BF)
    for copy in copies[4:]:
        copy.wait()


def start(right_sides, point_order, basis_in, leaf_map, *matrices):
    rows, columns = right_sides.shape
    rank = basis_in.shape[1]

    def block(count):
        return jax.ShapeDtypeStruct((count * rank, rank), BF)

    return pl.pallas_call(
        start_kernel,
        out_shape=(
            jax.ShapeDtypeStruct((SPREAD + 1,), jnp.int32),
            jax.ShapeDtypeStruct((rows, columns), BF),
            jax.ShapeDtypeStruct((rows, rank), BF),
            block(3),
            block(3),
            block(2),
            block(2),
            block(1),
            block(1),
        ),
        in_specs=[HBM] * 9,
        out_specs=(SMEM,) + (VMEM,) * 8,
        scratch_shapes=[
            pltpu.VMEM(right_sides.shape, BF),
            pltpu.VMEM(point_order.shape, jnp.int32),
            pltpu.VMEM(basis_in.shape, BF),
            pltpu.VMEM(right_sides.shape, F32),
            pltpu.SMEM(leaf_map.shape, jnp.int32),
            pltpu.SemaphoreType.DMA((16,)),
        ],
        compiler_params=params(),
        cost_estimate=took(2.7),
        name="start",
    )(*in_hbm(right_sides, point_order, basis_in, leaf_map, *matrices))


def invert_kernel(order_hbm, after, inv_ref, order, sem):
    copy = pltpu.make_async_copy(order_hbm, order, sem)
    copy.start()
    copy.wait()
    slot = order[...]
    columns = slot.shape[1]
    tiles = columns // LANES
    low = slot & (LANES - 1)
    high = slot // LANES
    here = lax.broadcasted_iota(jnp.int32, (tiles, columns), 1)
    mask = lax.broadcasted_iota(jnp.int32, (tiles, columns), 0) == high
    left = jnp.concatenate(
        [
            jnp.where(mask, (here // LANES).astype(F32), 0.0),
            jnp.where(mask, (here & (LANES - 1)).astype(F32), 0.0),
        ],
        0,
    ).astype(BF)
    right = (lax.broadcasted_iota(jnp.int32, (LANES, columns), 0) == low).astype(F32).astype(BF)
    both = lax.dot_general(left, right, (((1,), (1,)), ((), ())), preferred_element_type=F32)
    inv_ref[...] = (both[:tiles] * LANES + both[tiles:]).astype(jnp.int32)


def invert(point_order, after):
    columns = point_order.shape[1]
    return pl.pallas_call(
        invert_kernel,
        out_shape=jax.ShapeDtypeStruct((columns // LANES, LANES), jnp.int32),
        in_specs=[HBM, ANY],
        out_specs=VMEM,
        scratch_shapes=[pltpu.VMEM(point_order.shape, jnp.int32), pltpu.SemaphoreType.DMA],
        compiler_params=params(),
        cost_estimate=took(1.0),
        name="invert",
    )(*in_hbm(point_order), after)


def near_kernel(first, tree_ref, inverse_hbm, after, near_ref, held, sems):
    chunks, _, width = held.shape
    copies = [
        pltpu.make_async_copy(
            inverse_hbm.at[:, pl.ds(first + i * width, width)], held.at[i], sems.at[i]
        )
        for i in range(chunks)
    ]
    for copy in copies:
        copy.start()
    for i, copy in enumerate(copies):
        copy.wait()
        near_ref[:, i * width : (i + 1) * width] = mm(tree_ref[...], held[i])


def near_strip(tree, leaf_inverse, strip, strips, after):
    rows, columns = tree.shape
    width = columns // strips
    chunk = 2 * LANES
    chunks = width // chunk
    return pl.pallas_call(
        functools.partial(near_kernel, strip * width),
        out_shape=jax.ShapeDtypeStruct((rows, width), F32),
        in_specs=[VMEM, HBM, ANY],
        out_specs=VMEM,
        scratch_shapes=[
            pltpu.VMEM((chunks, columns, chunk), BF),
            pltpu.SemaphoreType.DMA((chunks,)),
        ],
        compiler_params=params(),
        cost_estimate=took(5.6 / strips),
        name="near",
    )(tree, *in_hbm(leaf_inverse), after)


def join_kernel(mine, other, after, out_ref):
    rows = mine.shape[0]
    out_ref[:rows] = mine[...]
    out_ref[rows:] = other[...]


def join(mine, other, after):
    rows, rank = mine.shape
    return pl.pallas_call(
        join_kernel,
        out_shape=jax.ShapeDtypeStruct((2 * rows, rank), BF),
        in_specs=[VMEM] * 2 + [ANY],
        out_specs=VMEM,
        compiler_params=params(),
        cost_estimate=took(0.1),
        name="join",
    )(mine, other, after)


def leaf_kernel(pick, pair_own, pair_x, up_ref, after, g0_ref, out_ref, table):
    rows = out_ref.shape[0]
    for m in range(SPREAD):
        pair = pair_own if m < 2 else pair_x
        table[m] = pair[m % 2 * rows : (m % 2 + 1) * rows]
    for m in range(SPREAD):
        g0_ref[m] = table[pick[m]]
    out_ref[...] = mm(g0_ref[0], up_ref[...])


def leaf_rise(pick, pair_own, pair_x, leaf_up, after):
    double, rank = pair_own.shape
    rows = double // 2
    return pl.pallas_call(
        leaf_kernel,
        out_shape=(
            jax.ShapeDtypeStruct((SPREAD, rows, rank), BF),
            jax.ShapeDtypeStruct((rows, rank), F32),
        ),
        in_specs=[SMEM] + [VMEM] * 3 + [ANY],
        out_specs=(VMEM,) * 2,
        scratch_shapes=[pltpu.VMEM((SPREAD, rows, rank), BF)],
        compiler_params=params(),
        cost_estimate=took(0.4),
        name="leaf_rise",
    )(pick, pair_own, pair_x, leaf_up, after)


def node_kernel(mine, other, maps_own, maps_in, after, out_ref):
    rows, rank = mine.shape
    g1 = (mine[...] + other[...]).astype(BF)
    out_ref[:rows] = g1
    out_ref[rows:] = mm(g1, held(0, maps_own, maps_in, 0, rank)).astype(BF)


def node_rise(mine, other, maps, after):
    rows, rank = mine.shape
    return pl.pallas_call(
        node_kernel,
        out_shape=jax.ShapeDtypeStruct((2 * rows, rank), BF),
        in_specs=[VMEM] * 4 + [ANY],
        out_specs=VMEM,
        compiler_params=params(),
        cost_estimate=took(0.2),
        name="node_rise",
    )(mine, other, *maps, after)


def level_kernel(bit, mine, other, maps_own, maps_in, after, sibling_ref, out_ref):
    rows = mine.shape[0] // 2
    rank = mine.shape[1]
    sibling_ref[...] = other[:rows]
    grown = (mine[rows:].astype(F32) + other[rows:].astype(F32)).astype(BF)
    out_ref[:rows] = grown
    out_ref[rows:] = mm(grown, held(bit, maps_own, maps_in, 0, rank)).astype(BF)


def level_rise(bit, mine, other, maps, after):
    double, rank = mine.shape
    return pl.pallas_call(
        functools.partial(level_kernel, bit),
        out_shape=(
            jax.ShapeDtypeStruct((double // 2, rank), BF),
            jax.ShapeDtypeStruct((double, rank), BF),
        ),
        in_specs=[VMEM] * 4 + [ANY],
        out_specs=(VMEM,) * 2,
        compiler_params=params(),
        cost_estimate=took(0.25),
        name="level_rise",
    )(mine, other, *maps, after)


def fall_kernel(low_bit, count, *refs):
    mine, other = refs[:2]
    siblings = refs[2 : 1 + count]
    owns = refs[1 + count : 2 + 2 * count]
    arrivals = refs[2 + 2 * count : 3 + 3 * count]
    out = refs[4 + 3 * count]
    rows = mine.shape[0] // 2
    rank = mine.shape[1]
    top = (mine[rows:].astype(F32) + other[rows:].astype(F32)).astype(BF)

    def part(k, begin):
        return held(low_bit + min(k, 1), owns[k], arrivals[k], begin, rank)

    value = mm(top, part(count, 0)).astype(BF)
    for k in range(count, 0, -1):
        sibling = other[:rows] if k == count else siblings[k - 1][...]
        cross = part(k, owns[k].shape[0] - rank)
        value = (mm(sibling, cross) + mm(value, part(k - 1, rank))).astype(BF)
    out[...] = value


def fall(low_bit, mine, other, siblings, maps, after):
    count = len(maps) - 1
    double, rank = mine.shape
    return pl.pallas_call(
        functools.partial(fall_kernel, low_bit, count),
        out_shape=jax.ShapeDtypeStruct((double // 2, rank), BF),
        in_specs=[VMEM] * (3 + 3 * count) + [ANY],
        out_specs=VMEM,
        compiler_params=params(),
        cost_estimate=took(0.45),
        name="fall",
    )(mine, other, *siblings, *[m[0] for m in maps], *[m[1] for m in maps], after)


def step_kernel(bit, mine, other, sibling, maps_own, maps_in, block_own, block_in, after, out):
    rank = mine.shape[1]
    value = jnp.where(bit_of_device(bit), other[...], mine[...])
    cross = held(bit, maps_own, maps_in, 2 * rank, rank)
    down = held(bit - 1, block_own, block_in, rank, rank)
    out[...] = (mm(sibling[...], cross) + mm(value, down)).astype(BF)


def step_down(bit, mine, other, sibling, maps, block_maps, after):
    rows, rank = mine.shape
    return pl.pallas_call(
        functools.partial(step_kernel, bit),
        out_shape=jax.ShapeDtypeStruct((rows, rank), BF),
        in_specs=[VMEM] * 7 + [ANY],
        out_specs=VMEM,
        compiler_params=params(),
        cost_estimate=took(0.2),
        name="step_down",
    )(mine, other, sibling, *maps, *block_maps, after)


def local_kernel(g0_ref, node_pay, node_own, node_in, block_own, block_in, cross_in, down_ref, after, out_ref):
    rank = down_ref.shape[0]
    rows = node_pay.shape[0] // 2
    cross = held(1, block_own, block_in, 2 * rank, rank)
    cross = jnp.where(bit_of_device(0), cross_in[...], cross)
    inner = mm(node_pay[:rows], cross).astype(BF)
    out_ref[:rank] = mm(held(0, node_own, node_in, rank, rank), down_ref[...]).astype(BF)
    nearest = held(0, node_own, node_in, 2 * rank, rank)
    out_ref[rank:] = (mm(g0_ref[1], nearest) + mm(inner, down_ref[...])).astype(BF)


def local(g0, node_pay, node_maps, block_maps, block_cross, leaf_down, after):
    _, rows, rank = g0.shape
    return pl.pallas_call(
        local_kernel,
        out_shape=jax.ShapeDtypeStruct((rank + rows, rank), BF),
        in_specs=[VMEM] * 8 + [ANY],
        out_specs=VMEM,
        compiler_params=params(),
        cost_estimate=took(0.6),
        name="local",
    )(g0, node_pay, *node_maps, *block_maps, block_cross, leaf_down, after)


def choose_kernel(bit, upper, lower, after, out_ref):
    out_ref[...] = held(bit, upper, lower, 0, out_ref.shape[0])


def choose(bit, upper, lower, after):
    return pl.pallas_call(
        functools.partial(choose_kernel, bit),
        out_shape=jax.ShapeDtypeStruct(upper.shape, BF),
        in_specs=[VMEM] * 2 + [ANY],
        out_specs=VMEM,
        compiler_params=params(),
        cost_estimate=took(0.2),
        name="choose",
    )(upper, lower, after)


def final_kernel(strips, pick, f_own, f_core, l0, l1, l2, l3, out_basis, inv_ref, *refs):
    nears = refs[:strips]
    answer, total, leaf_f = refs[strips:]
    rank = f_own.shape[1]
    f2 = jnp.where(bit_of_device(0), f_core[...], f_own[...])
    for m, pack_ref in enumerate((l0, l1, l2, l3)):

        @pl.when(pick[SPREAD] == m)
        def _():
            leaf_f[...] = (mm(f2, pack_ref[:rank, :]) + pack_ref[rank:, :].astype(F32)).astype(BF)

    width = nears[0].shape[1]
    for i in range(strips):
        span = slice(i * width, (i + 1) * width)
        total[:, span] = nears[i][...] + mm(leaf_f[...], out_basis[:, span])

    def store(tile, found):
        answer[:, tile * LANES : (tile + 1) * LANES] = found

    gather_columns(total, lambda tile: inv_ref[tile : tile + 1, :], store)


def final(pick, f2, f2_core, locals_, basis_out, inverse_order, nears):
    rows, rank = f2.shape
    columns = basis_out.shape[1]
    return pl.pallas_call(
        functools.partial(final_kernel, len(nears)),
        out_shape=jax.ShapeDtypeStruct((rows, columns), F32),
        in_specs=[SMEM] + [VMEM] * (8 + len(nears)),
        out_specs=VMEM,
        scratch_shapes=[pltpu.VMEM((rows, columns), F32), pltpu.VMEM((rows, rank), BF)],
        compiler_params=params(),
        cost_estimate=took(2.9),
        name="final",
    )(pick, f2, f2_core, *locals_, basis_out, inverse_order, *nears)


def body(
    right_sides,
    point_order,
    leaf_inverse,
    basis_in,
    basis_out,
    leaf_up,
    leaf_down,
    node_up,
    node_down,
    node_cross,
    leaf_map,
):
    members = lax.axis_size("leaf")
    levels = members.bit_length() - 1
    cut = SPREAD.bit_length() - 1
    me = lax.axis_index("leaf")
    rank = leaf_up.shape[1]
    offset = me & (SPREAD - 1)

    def to_left(block, bit):
        step = 1 << bit
        return lax.ppermute(block, "leaf", [(i + step, i) for i in range(0, members, 2 * step)])

    def to_right(block, bit, every):
        step = 1 << bit
        pairs = [(i, i + step) for i in range(0, members, every) if i & step == 0]
        return lax.ppermute(block, "leaf", pairs)

    pick, tree, reduced, low, high, top_low, top_high, up_map, down_map = start(
        right_sides, point_order, basis_in, leaf_map, leaf_up, leaf_down, node_up, node_down, node_cross
    )
    node_maps = (high, to_left(low, 0))
    block_maps = (high, to_left(low, 1))
    held_maps = []
    for level in range(cut + 1, levels + 1):
        first, second = (top_low, top_high) if level == levels else (low, high)
        held_maps.append((second, to_left(first, level - 1)))

    pair = join(reduced, swap(reduced, 1), reduced)
    g0, product = leaf_rise(pick, pair, swap(pair, 2), up_map, pair)
    pay = node_rise(product, swap(product, 1), node_maps, product)
    node_in = swap(pay, 2)
    siblings = []
    near0 = near1 = None
    for bit in range(1, levels - 1):
        arrived = node_in if bit == 1 else swap(pay, 1 << bit)
        after = pay
        if bit == 2:
            near0 = after = near_strip(tree, leaf_inverse, 0, 2, pay)
            block_cross = choose(1, high[2 * rank :], block_maps[1][2 * rank :], pay)
            block_cross = to_right(block_cross, 0, 2)
        if bit == cut + 1:
            for level in range(cut + 3, levels + 1):
                own, passed = held_maps[level - cut - 1]
                now = choose(level - 1, own, passed, pay)
                for step in range(level - 2, cut, -1):
                    passed = to_right(now, step, 1 << step)
                    if step > cut + 1:
                        now = choose(step, passed, now, pay)
                held_maps[level - cut - 1] = (passed, now)
        if bit == 3:
            own_local = after = local(
                g0, node_in, node_maps, block_maps, block_cross, down_map, pay
            )
        maps = block_maps if bit == 1 else held_maps[bit - cut]
        sibling, pay = level_rise(min(bit, cut + 1), pay, arrived, maps, after)
        siblings.append(sibling)

    local_x = swap(own_local, 2)
    locals_ = [own_local, swap(own_local, 1), local_x, swap(local_x, 1)]
    near1 = near_strip(tree, leaf_inverse, 1, 2, pay)

    cut_f = fall(cut, pay, swap(pay, 1 << (levels - 1)), siblings[2:], held_maps, near1)
    inverse_order = invert(point_order, cut_f)
    block_f = step_down(
        cut, cut_f, swap(cut_f, SPREAD), siblings[1], held_maps[0], block_maps, inverse_order
    )
    from_x = swap(block_f, 2)
    block_f = jnp.where(offset & 2 != 0, from_x, block_f)
    return final(
        pick, block_f, swap(block_f, 1), locals_, basis_out, inverse_order, [near0, near1]
    )


def solution(mesh):
    placed = (
        P(None, "leaf"),
        P("leaf", None),
        P("leaf", None),
        P("leaf", None),
        P("leaf", None),
        P("leaf", None),
        P("leaf", None),
        P("leaf", None),
        P("leaf", None),
        P("leaf", None),
        P(),
    )
    return jax.shard_map(
        body, mesh=mesh, in_specs=placed, out_specs=P(None, "leaf"), check_vma=False
    )
```

```python
import functools

import jax
import jax.numpy as jnp
from jax import lax
from jax.experimental import pallas as pl
from jax.experimental.pallas import tpu as pltpu
from jax.sharding import PartitionSpec as P

SPREAD = 4
LANES = 128
BF = jnp.bfloat16
F32 = jnp.float32
VMEM = pl.BlockSpec(memory_space=pltpu.VMEM)
ANY = pl.BlockSpec(memory_space=pl.ANY)
HBM = pl.BlockSpec(memory_space=pltpu.HBM)
LIMIT = 32 * 2**20


def mm(a, b):
    return jnp.dot(a, b, preferred_element_type=F32)


def params():
    return pltpu.CompilerParams(vmem_limit_bytes=LIMIT)


def in_hbm(*arrays):
    return [pltpu.with_memory_space_constraint(array, pltpu.HBM) for array in arrays]


def took(micros):
    return pl.CostEstimate(flops=0, bytes_accessed=int(micros * 3e6), transcendentals=0)


def swap(block, mask):
    count = lax.axis_size("leaf")
    return lax.ppermute(block, "leaf", [(i, i ^ mask) for i in range(count)])


def bit_of_device(bit):
    return (lax.axis_index("leaf").astype(jnp.int32) & (1 << bit)) != 0


def picked(number, choices):
    number = number[:, :1]
    result = choices[0]
    for m in range(1, len(choices)):
        result = jnp.where(number == m, choices[m], result)
    return result


def held(bit, own, arrived, begin, size):
    rows = slice(begin, begin + size)
    if own is arrived:
        return own[rows, :]
    return jnp.where(bit_of_device(bit), own[rows, :], arrived[rows, :])


def gather_columns(table, slots, store):
    rows, columns = table.shape
    tiles = columns // LANES
    for out_tile in range(tiles):
        slot = jnp.broadcast_to(slots(out_tile), (rows, LANES))
        low = slot & (LANES - 1)
        high = slot // LANES
        found = None
        for tile in range(tiles):
            part = jnp.take_along_axis(
                table[:, tile * LANES : (tile + 1) * LANES], low, axis=1
            )
            found = part if found is None else jnp.where(high == tile, part, found)
        store(out_tile, found)


def start_kernel(rhs_hbm, order_hbm, basis_hbm, map_hbm, leaf_up, leaf_down, node_up, node_down, node_cross,
                 pick, tree_ref, red_ref, low_ref, high_ref, toplow_ref, tophigh_ref, up_ref, down_ref,
                 rhs, order, basis, table, seats, sems):
    rank = red_ref.shape[1]
    cross_low = node_cross.at[pl.ds(0, rank), :]
    cross_high = node_cross.at[pl.ds(rank, rank), :]
    copies = [
        pltpu.make_async_copy(rhs_hbm, rhs, sems.at[0]),
        pltpu.make_async_copy(order_hbm, order, sems.at[1]),
        pltpu.make_async_copy(map_hbm, seats, sems.at[2]),
        pltpu.make_async_copy(basis_hbm, basis, sems.at[3]),
    ]
    packs = (
        (low_ref, (node_up, node_down, cross_low)),
        (high_ref, (node_up, node_down, cross_high)),
        (toplow_ref, (node_up, cross_low)),
        (tophigh_ref, (node_up, cross_high)),
        (up_ref, (leaf_up,)),
        (down_ref, (leaf_down,)),
    )
    for dst, parts in packs:
        for i, part in enumerate(parts):
            copies.append(
                pltpu.make_async_copy(
                    part, dst.at[pl.ds(i * rank, rank), :], sems.at[len(copies)]
                )
            )
    for copy in copies:
        copy.start()
    copies[2].wait()
    me = lax.axis_index("leaf").astype(jnp.int32)
    offset = me & (SPREAD - 1)
    base = me - offset
    placed = [seats[base + slot] & (SPREAD - 1) for slot in range(SPREAD)]
    seat = placed[0]
    for slot in range(1, SPREAD):
        seat = jnp.where(offset == slot, placed[slot], seat)
    for m in range(SPREAD):
        source = jnp.int32(0)
        for slot in range(1, SPREAD):
            source = jnp.where(placed[slot] == (offset ^ m), slot, source)
        pick[m : m + 1, :] = jnp.full((1, LANES), source ^ offset, jnp.int32)
    pick[SPREAD : SPREAD + 1, :] = jnp.full((1, LANES), seat ^ offset, jnp.int32)
    copies[0].wait()
    table[...] = rhs[...].astype(F32)
    copies[1].wait()

    def store(tile, found):
        tree_ref[:, tile * LANES : (tile + 1) * LANES] = found.astype(BF)

    gather_columns(
        table, lambda tile: order[:, tile * LANES : (tile + 1) * LANES], store
    )
    copies[3].wait()
    red_ref[...] = mm(tree_ref[...], basis[...]).astype(BF)
    for copy in copies[4:]:
        copy.wait()


def start(right_sides, point_order, basis_in, leaf_map, *matrices):
    rows, columns = right_sides.shape
    rank = basis_in.shape[1]

    def block(count):
        return jax.ShapeDtypeStruct((count * rank, rank), BF)

    return pl.pallas_call(
        start_kernel,
        out_shape=(
            jax.ShapeDtypeStruct((2 * SPREAD, LANES), jnp.int32),
            jax.ShapeDtypeStruct((rows, columns), BF),
            jax.ShapeDtypeStruct((rows, rank), BF),
            block(3),
            block(3),
            block(2),
            block(2),
            block(1),
            block(1),
        ),
        in_specs=[HBM] * 9,
        out_specs=(VMEM,) * 9,
        scratch_shapes=[
            pltpu.VMEM(right_sides.shape, BF),
            pltpu.VMEM(point_order.shape, jnp.int32),
            pltpu.VMEM(basis_in.shape, BF),
            pltpu.VMEM(right_sides.shape, F32),
            pltpu.SMEM(leaf_map.shape, jnp.int32),
            pltpu.SemaphoreType.DMA((16,)),
        ],
        compiler_params=params(),
        cost_estimate=took(2.7),
        name="start",
    )(*in_hbm(right_sides, point_order, basis_in, leaf_map, *matrices))


def invert_kernel(order_hbm, after, inv_ref, order, sem):
    copy = pltpu.make_async_copy(order_hbm, order, sem)
    copy.start()
    copy.wait()
    slot = order[...]
    columns = slot.shape[1]
    tiles = columns // LANES
    low = slot & (LANES - 1)
    high = slot // LANES
    here = lax.broadcasted_iota(jnp.int32, (tiles, columns), 1)
    mask = lax.broadcasted_iota(jnp.int32, (tiles, columns), 0) == high
    left = jnp.concatenate(
        [
            jnp.where(mask, (here // LANES).astype(F32), 0.0),
            jnp.where(mask, (here & (LANES - 1)).astype(F32), 0.0),
        ],
        0,
    ).astype(BF)
    right = (lax.broadcasted_iota(jnp.int32, (LANES, columns), 0) == low).astype(F32).astype(BF)
    both = lax.dot_general(left, right, (((1,), (1,)), ((), ())), preferred_element_type=F32)
    inv_ref[...] = (both[:tiles] * LANES + both[tiles:]).astype(jnp.int32)


def invert(point_order, after):
    columns = point_order.shape[1]
    return pl.pallas_call(
        invert_kernel,
        out_shape=jax.ShapeDtypeStruct((columns // LANES, LANES), jnp.int32),
        in_specs=[HBM, ANY],
        out_specs=VMEM,
        scratch_shapes=[pltpu.VMEM(point_order.shape, jnp.int32), pltpu.SemaphoreType.DMA],
        compiler_params=params(),
        cost_estimate=took(1.0),
        name="invert",
    )(*in_hbm(point_order), after)


def near_kernel(first, tree_ref, inverse_hbm, after, near_ref, held, sems):
    chunks, _, width = held.shape
    copies = [
        pltpu.make_async_copy(
            inverse_hbm.at[:, pl.ds(first + i * width, width)], held.at[i], sems.at[i]
        )
        for i in range(chunks)
    ]
    for copy in copies:
        copy.start()
    for i, copy in enumerate(copies):
        copy.wait()
        near_ref[:, i * width : (i + 1) * width] = mm(tree_ref[...], held[i])


def near_strip(tree, leaf_inverse, strip, strips, after):
    rows, columns = tree.shape
    width = columns // strips
    chunk = 2 * LANES
    chunks = width // chunk
    return pl.pallas_call(
        functools.partial(near_kernel, strip * width),
        out_shape=jax.ShapeDtypeStruct((rows, width), F32),
        in_specs=[VMEM, HBM, ANY],
        out_specs=VMEM,
        scratch_shapes=[
            pltpu.VMEM((chunks, columns, chunk), BF),
            pltpu.SemaphoreType.DMA((chunks,)),
        ],
        compiler_params=params(),
        cost_estimate=took(5.6 / strips),
        name="near",
    )(tree, *in_hbm(leaf_inverse), after)


def join_kernel(mine, other, after, out_ref):
    rows = mine.shape[0]
    out_ref[:rows] = mine[...]
    out_ref[rows:] = other[...]


def join(mine, other, after):
    rows, rank = mine.shape
    return pl.pallas_call(
        join_kernel,
        out_shape=jax.ShapeDtypeStruct((2 * rows, rank), BF),
        in_specs=[VMEM] * 2 + [ANY],
        out_specs=VMEM,
        compiler_params=params(),
        cost_estimate=took(0.1),
        name="join",
    )(mine, other, after)


def leaf_kernel(pick, pair_own, pair_x, up_ref, after, g0_ref, out_ref):
    rows = out_ref.shape[0]
    table = [
        pair[m * rows : (m + 1) * rows, :].astype(F32) for pair in (pair_own, pair_x) for m in (0, 1)
    ]
    for m in range(SPREAD):
        g0_ref[m] = picked(pick[m : m + 1, :], table).astype(BF)
    out_ref[...] = mm(g0_ref[0], up_ref[...])


def leaf_rise(pick, pair_own, pair_x, leaf_up, after):
    double, rank = pair_own.shape
    rows = double // 2
    return pl.pallas_call(
        leaf_kernel,
        out_shape=(
            jax.ShapeDtypeStruct((SPREAD, rows, rank), BF),
            jax.ShapeDtypeStruct((rows, rank), F32),
        ),
        in_specs=[VMEM] * 4 + [ANY],
        out_specs=(VMEM,) * 2,
        compiler_params=params(),
        cost_estimate=took(0.4),
        name="leaf_rise",
    )(pick, pair_own, pair_x, leaf_up, after)


def node_kernel(mine, other, maps_own, maps_in, after, out_ref):
    rows, rank = mine.shape
    g1 = (mine[...] + other[...]).astype(BF)
    out_ref[:rows] = g1
    out_ref[rows:] = mm(g1, held(0, maps_own, maps_in, 0, rank)).astype(BF)


def node_rise(mine, other, maps, after):
    rows, rank = mine.shape
    return pl.pallas_call(
        node_kernel,
        out_shape=jax.ShapeDtypeStruct((2 * rows, rank), BF),
        in_specs=[VMEM] * 4 + [ANY],
        out_specs=VMEM,
        compiler_params=params(),
        cost_estimate=took(0.2),
        name="node_rise",
    )(mine, other, *maps, after)


def level_kernel(bit, mine, other, maps_own, maps_in, after, out_ref):
    rows = mine.shape[0] // 2
    rank = mine.shape[1]
    grown = (mine[rows:].astype(F32) + other[rows:].astype(F32)).astype(BF)
    out_ref[:rows] = grown
    out_ref[rows:] = mm(grown, held(bit, maps_own, maps_in, 0, rank)).astype(BF)


def level_rise(bit, mine, other, maps, after):
    double, rank = mine.shape
    return pl.pallas_call(
        functools.partial(level_kernel, bit),
        out_shape=jax.ShapeDtypeStruct((double, rank), BF),
        in_specs=[VMEM] * 4 + [ANY],
        out_specs=VMEM,
        compiler_params=params(),
        cost_estimate=took(0.25),
        name="level_rise",
    )(mine, other, *maps, after)


def fall_kernel(low_bit, count, *refs):
    mine, other = refs[:2]
    siblings = refs[2 : 1 + count]
    owns = refs[1 + count : 2 + 2 * count]
    arrivals = refs[2 + 2 * count : 3 + 3 * count]
    out = refs[4 + 3 * count]
    rows = mine.shape[0] // 2
    rank = mine.shape[1]
    top = (mine[rows:].astype(F32) + other[rows:].astype(F32)).astype(BF)

    def part(k, begin):
        return held(low_bit + min(k, 1), owns[k], arrivals[k], begin, rank)

    value = mm(top, part(count, 0)).astype(BF)
    for k in range(count, 0, -1):
        sibling = other[:rows] if k == count else siblings[k - 1][:rows]
        cross = part(k, owns[k].shape[0] - rank)
        value = (mm(sibling, cross) + mm(value, part(k - 1, rank))).astype(BF)
    out[...] = value


def fall(low_bit, mine, other, siblings, maps, after):
    count = len(maps) - 1
    double, rank = mine.shape
    return pl.pallas_call(
        functools.partial(fall_kernel, low_bit, count),
        out_shape=jax.ShapeDtypeStruct((double // 2, rank), BF),
        in_specs=[VMEM] * (3 + 3 * count) + [ANY],
        out_specs=VMEM,
        compiler_params=params(),
        cost_estimate=took(0.45),
        name="fall",
    )(mine, other, *siblings, *[m[0] for m in maps], *[m[1] for m in maps], after)


def step_kernel(bit, mine, other, sibling, maps_own, maps_in, block_own, block_in, after, out):
    rank = mine.shape[1]
    value = jnp.where(bit_of_device(bit), other[...], mine[...])
    cross = held(bit, maps_own, maps_in, 2 * rank, rank)
    down = held(bit - 1, block_own, block_in, rank, rank)
    out[...] = (mm(sibling[: mine.shape[0]], cross) + mm(value, down)).astype(BF)


def step_down(bit, mine, other, sibling, maps, block_maps, after):
    rows, rank = mine.shape
    return pl.pallas_call(
        functools.partial(step_kernel, bit),
        out_shape=jax.ShapeDtypeStruct((rows, rank), BF),
        in_specs=[VMEM] * 7 + [ANY],
        out_specs=VMEM,
        compiler_params=params(),
        cost_estimate=took(0.2),
        name="step_down",
    )(mine, other, sibling, *maps, *block_maps, after)


def local_kernel(g0_ref, node_pay, node_own, node_in, block_own, block_in, cross_in, down_ref, after, out_ref):
    rank = down_ref.shape[0]
    rows = node_pay.shape[0] // 2
    cross = held(1, block_own, block_in, 2 * rank, rank)
    cross = jnp.where(bit_of_device(0), cross_in[...], cross)
    inner = mm(node_pay[:rows], cross).astype(BF)
    out_ref[:rank] = mm(held(0, node_own, node_in, rank, rank), down_ref[...]).astype(BF)
    nearest = held(0, node_own, node_in, 2 * rank, rank)
    out_ref[rank:] = (mm(g0_ref[1], nearest) + mm(inner, down_ref[...])).astype(BF)


def local(g0, node_pay, node_maps, block_maps, block_cross, leaf_down, after):
    _, rows, rank = g0.shape
    return pl.pallas_call(
        local_kernel,
        out_shape=jax.ShapeDtypeStruct((rank + rows, rank), BF),
        in_specs=[VMEM] * 8 + [ANY],
        out_specs=VMEM,
        compiler_params=params(),
        cost_estimate=took(0.6),
        name="local",
    )(g0, node_pay, *node_maps, *block_maps, block_cross, leaf_down, after)


def choose_kernel(bit, upper, lower, after, out_ref):
    out_ref[...] = held(bit, upper, lower, 0, out_ref.shape[0])


def pass_kernel(block, after, out_ref):
    out_ref[...] = block[...]


def pass_on(block, after):
    return pl.pallas_call(
        pass_kernel,
        out_shape=jax.ShapeDtypeStruct(block.shape, block.dtype),
        in_specs=[VMEM, ANY],
        out_specs=VMEM,
        compiler_params=params(),
        cost_estimate=took(0.2),
        name="pass_on",
    )(block, after)


def choose(bit, upper, lower, after):
    return pl.pallas_call(
        functools.partial(choose_kernel, bit),
        out_shape=jax.ShapeDtypeStruct(upper.shape, BF),
        in_specs=[VMEM] * 2 + [ANY],
        out_specs=VMEM,
        compiler_params=params(),
        cost_estimate=took(0.2),
        name="choose",
    )(upper, lower, after)


def final_kernel(strips, pick, f_own, f_core, l0, l1, l2, l3, out_basis, inv_ref, *refs):
    nears = refs[:strips]
    answer_hbm, total, answer, sems = refs[strips:]
    rank = f_own.shape[1]
    f2 = jnp.where(bit_of_device(0), f_core[...], f_own[...])
    values = [
        mm(f2, pack_ref[:rank, :]) + pack_ref[rank:, :].astype(F32) for pack_ref in (l0, l1, l2, l3)
    ]
    leaf_f = picked(pick[SPREAD : SPREAD + 1, :], values).astype(BF)
    width = nears[0].shape[1]
    for i in range(strips):
        span = slice(i * width, (i + 1) * width)
        total[:, span] = nears[i][...] + mm(leaf_f, out_basis[:, span])

    copies = []

    def store(tile, found):
        answer[:, tile * LANES : (tile + 1) * LANES] = found
        if tile % 4 == 3:
            span = pl.ds((tile - 3) * LANES, 4 * LANES)
            copies.append(
                pltpu.make_async_copy(
                    answer.at[:, span], answer_hbm.at[:, span], sems.at[len(copies)]
                )
            )
            copies[-1].start()

    gather_columns(total, lambda tile: inv_ref[tile : tile + 1, :], store)
    for copy in copies:
        copy.wait()


def final(pick, f2, f2_core, locals_, basis_out, inverse_order, nears):
    rows, rank = f2.shape
    columns = basis_out.shape[1]
    return pl.pallas_call(
        functools.partial(final_kernel, len(nears)),
        out_shape=jax.ShapeDtypeStruct((rows, columns), F32),
        in_specs=[VMEM] * (9 + len(nears)),
        out_specs=ANY,
        scratch_shapes=[
            pltpu.VMEM((rows, columns), F32),
            pltpu.VMEM((rows, columns), F32),
            pltpu.SemaphoreType.DMA((columns // (4 * LANES),)),
        ],
        compiler_params=params(),
        cost_estimate=took(2.9),
        name="final",
    )(pick, f2, f2_core, *locals_, basis_out, inverse_order, *nears)


def body(
    right_sides,
    point_order,
    leaf_inverse,
    basis_in,
    basis_out,
    leaf_up,
    leaf_down,
    node_up,
    node_down,
    node_cross,
    leaf_map,
):
    members = lax.axis_size("leaf")
    levels = members.bit_length() - 1
    cut = SPREAD.bit_length() - 1
    me = lax.axis_index("leaf")
    rank = leaf_up.shape[1]
    offset = me & (SPREAD - 1)

    def cycle(bit):
        step = 1 << bit
        pairs = []
        for i in range(0, members, 2):
            if i & step == 0:
                pairs += [(i + step, i), (i, i | 1), (i | 1, (i + step) | 1), ((i + step) | 1, i + step)]
        return pairs

    def to_left(block, bit):
        if bit == 0:
            return swap(block, 1)
        return lax.ppermute(block, "leaf", cycle(bit))

    def to_right(block, bit):
        if bit == 0:
            return swap(block, 1)
        return lax.ppermute(block, "leaf", [(j, i) for i, j in cycle(bit)])

    pick, tree, reduced, low, high, top_low, top_high, up_map, down_map = start(
        right_sides, point_order, basis_in, leaf_map, leaf_up, leaf_down, node_up, node_down, node_cross
    )
    node_maps = (high, to_left(low, 0))

    pair = join(reduced, swap(reduced, 1), reduced)
    gate = pass_on(low, pair)
    block_maps = (high, to_left(gate, 1))
    g0, product = leaf_rise(pick, pair, swap(pair, 2), up_map, gate)
    gate = pass_on(low, product)
    held_maps = [(high, to_left(gate, cut))]
    pay = node_rise(product, swap(product, 1), node_maps, gate)
    for level in range(levels, cut + 1, -1):
        first, second = (top_low, top_high) if level == levels else (low, high)
        gate = pass_on(first, pay)
        held_maps.insert(1, (second, to_left(gate, level - 1)))
    strips = 4
    nears = []
    arrivals = []
    for bit in range(1, levels - 1):
        arrivals.append(swap(pay, 1 << bit))
        if bit <= cut:
            after = near_strip(tree, leaf_inverse, len(nears), strips, pay)
            nears.append(after)
        if bit == cut + 1:
            after = pay
            for level in range(cut + 3, levels + 1):
                own, passed = held_maps[level - cut - 1]
                now = after = choose(level - 1, own, passed, pay)
                for step in range(level - 2, cut, -1):
                    passed = to_right(now, step)
                    if step > cut + 1:
                        now = choose(step, passed, now, pay)
                held_maps[level - cut - 1] = (passed, now)
        maps = block_maps if bit == 1 else held_maps[bit - cut]
        pay = level_rise(min(bit, cut + 1), pay, arrivals[-1], maps, after)
        if bit == cut:
            block_cross = choose(1, high[2 * rank :], block_maps[1][2 * rank :], pay)
            block_cross = to_right(block_cross, 0)

    own_local = local(g0, arrivals[0], node_maps, block_maps, block_cross, down_map, pay)
    local_x = swap(own_local, 2)
    nears.append(near_strip(tree, leaf_inverse, 2, strips, own_local))

    cut_f = fall(cut, pay, swap(pay, 1 << (levels - 1)), arrivals[2:], held_maps, nears[2])
    nears.append(near_strip(tree, leaf_inverse, 3, strips, cut_f))
    block_f = step_down(
        cut, cut_f, swap(cut_f, SPREAD), arrivals[1], held_maps[0], block_maps, nears[3]
    )
    inverse_order = invert(point_order, block_f)
    locals_ = [own_local, swap(own_local, 1), local_x, swap(pass_on(local_x, block_f), 1)]
    block_f = choose(1, swap(block_f, 2), block_f, inverse_order)
    return final(
        pick, block_f, swap(block_f, 1), locals_, basis_out, inverse_order, nears
    )


def solution(mesh):
    placed = (
        P(None, "leaf"),
        P("leaf", None),
        P("leaf", None),
        P("leaf", None),
        P("leaf", None),
        P("leaf", None),
        P("leaf", None),
        P("leaf", None),
        P("leaf", None),
        P("leaf", None),
        P(),
    )
    return jax.shard_map(
        body, mesh=mesh, in_specs=placed, out_specs=P(None, "leaf"), check_vma=False
    )
```

```python
import functools

import jax
import jax.numpy as jnp
from jax import lax
from jax.experimental import pallas as pl
from jax.experimental.pallas import tpu as pltpu
from jax.sharding import PartitionSpec as P

SPREAD = 4
LANES = 128
BF = jnp.bfloat16
F32 = jnp.float32
VMEM = pl.BlockSpec(memory_space=pltpu.VMEM)
ANY = pl.BlockSpec(memory_space=pl.ANY)
HBM = pl.BlockSpec(memory_space=pltpu.HBM)
LIMIT = 32 * 2**20


def mm(a, b):
    return jnp.dot(a, b, preferred_element_type=F32)


def params():
    return pltpu.CompilerParams(vmem_limit_bytes=LIMIT)


def in_hbm(*arrays):
    return [pltpu.with_memory_space_constraint(array, pltpu.HBM) for array in arrays]


def took(micros):
    return pl.CostEstimate(flops=0, bytes_accessed=int(micros * 3e6), transcendentals=0)


def swap(block, mask):
    count = lax.axis_size("leaf")
    return lax.ppermute(block, "leaf", [(i, i ^ mask) for i in range(count)])


def bit_of_device(bit):
    return (lax.axis_index("leaf").astype(jnp.int32) & (1 << bit)) != 0


def picked(number, choices):
    number = number[:, :1]
    result = choices[0]
    for m in range(1, len(choices)):
        result = jnp.where(number == m, choices[m], result)
    return result


def held(bit, own, arrived, begin, size):
    rows = slice(begin, begin + size)
    if own is arrived:
        return own[rows, :]
    return jnp.where(bit_of_device(bit), own[rows, :], arrived[rows, :])


def gather_columns(table, slots, store):
    rows, columns = table.shape
    tiles = columns // LANES
    for out_tile in range(tiles):
        slot = jnp.broadcast_to(slots(out_tile), (rows, LANES))
        low = slot & (LANES - 1)
        high = slot // LANES
        found = None
        for tile in range(tiles):
            part = jnp.take_along_axis(
                table[:, tile * LANES : (tile + 1) * LANES], low, axis=1
            )
            found = part if found is None else jnp.where(high == tile, part, found)
        store(out_tile, found)


def start_kernel(rhs_hbm, order_hbm, basis_hbm, map_hbm, leaf_up, leaf_down, node_up, node_down, node_cross,
                 pick, tree_ref, red_ref, low_ref, high_ref, toplow_ref, tophigh_ref, up_ref, down_ref,
                 rhs, order, basis, table, seats, sems):
    rank = red_ref.shape[1]
    cross_low = node_cross.at[pl.ds(0, rank), :]
    cross_high = node_cross.at[pl.ds(rank, rank), :]
    copies = [
        pltpu.make_async_copy(rhs_hbm, rhs, sems.at[0]),
        pltpu.make_async_copy(order_hbm, order, sems.at[1]),
        pltpu.make_async_copy(map_hbm, seats, sems.at[2]),
        pltpu.make_async_copy(basis_hbm, basis, sems.at[3]),
    ]
    packs = (
        (low_ref, (node_up, node_down, cross_low)),
        (high_ref, (node_up, node_down, cross_high)),
        (toplow_ref, (node_up, cross_low)),
        (tophigh_ref, (node_up, cross_high)),
        (up_ref, (leaf_up,)),
        (down_ref, (leaf_down,)),
    )
    for dst, parts in packs:
        for i, part in enumerate(parts):
            copies.append(
                pltpu.make_async_copy(
                    part, dst.at[pl.ds(i * rank, rank), :], sems.at[len(copies)]
                )
            )
    for copy in copies:
        copy.start()
    copies[2].wait()
    me = lax.axis_index("leaf").astype(jnp.int32)
    offset = me & (SPREAD - 1)
    base = me - offset
    placed = [seats[base + slot] & (SPREAD - 1) for slot in range(SPREAD)]
    seat = placed[0]
    for slot in range(1, SPREAD):
        seat = jnp.where(offset == slot, placed[slot], seat)
    for m in range(SPREAD):
        source = jnp.int32(0)
        for slot in range(1, SPREAD):
            source = jnp.where(placed[slot] == (offset ^ m), slot, source)
        pick[m : m + 1, :] = jnp.full((1, LANES), source ^ offset, jnp.int32)
    pick[SPREAD : SPREAD + 1, :] = jnp.full((1, LANES), seat ^ offset, jnp.int32)
    copies[0].wait()
    table[...] = rhs[...].astype(F32)
    copies[1].wait()

    def store(tile, found):
        tree_ref[:, tile * LANES : (tile + 1) * LANES] = found.astype(BF)

    gather_columns(
        table, lambda tile: order[:, tile * LANES : (tile + 1) * LANES], store
    )
    copies[3].wait()
    red_ref[...] = mm(tree_ref[...], basis[...]).astype(BF)
    for copy in copies[4:]:
        copy.wait()


def start(right_sides, point_order, basis_in, leaf_map, *matrices):
    rows, columns = right_sides.shape
    rank = basis_in.shape[1]

    def block(count):
        return jax.ShapeDtypeStruct((count * rank, rank), BF)

    return pl.pallas_call(
        start_kernel,
        out_shape=(
            jax.ShapeDtypeStruct((2 * SPREAD, LANES), jnp.int32),
            jax.ShapeDtypeStruct((rows, columns), BF),
            jax.ShapeDtypeStruct((rows, rank), BF),
            block(3),
            block(3),
            block(2),
            block(2),
            block(1),
            block(1),
        ),
        in_specs=[HBM] * 9,
        out_specs=(VMEM,) * 9,
        scratch_shapes=[
            pltpu.VMEM(right_sides.shape, BF),
            pltpu.VMEM(point_order.shape, jnp.int32),
            pltpu.VMEM(basis_in.shape, BF),
            pltpu.VMEM(right_sides.shape, F32),
            pltpu.SMEM(leaf_map.shape, jnp.int32),
            pltpu.SemaphoreType.DMA((16,)),
        ],
        compiler_params=params(),
        cost_estimate=took(2.7),
        name="start",
    )(*in_hbm(right_sides, point_order, basis_in, leaf_map, *matrices))


def invert_kernel(order_hbm, after, inv_ref, order, sem):
    copy = pltpu.make_async_copy(order_hbm, order, sem)
    copy.start()
    copy.wait()
    slot = order[...]
    columns = slot.shape[1]
    tiles = columns // LANES
    low = slot & (LANES - 1)
    high = slot // LANES
    here = lax.broadcasted_iota(jnp.int32, (tiles, columns), 1)
    mask = lax.broadcasted_iota(jnp.int32, (tiles, columns), 0) == high
    left = jnp.concatenate(
        [
            jnp.where(mask, (here // LANES).astype(F32), 0.0),
            jnp.where(mask, (here & (LANES - 1)).astype(F32), 0.0),
        ],
        0,
    ).astype(BF)
    right = (lax.broadcasted_iota(jnp.int32, (LANES, columns), 0) == low).astype(F32).astype(BF)
    both = lax.dot_general(left, right, (((1,), (1,)), ((), ())), preferred_element_type=F32)
    inv_ref[...] = (both[:tiles] * LANES + both[tiles:]).astype(jnp.int32)


def invert(point_order, after):
    columns = point_order.shape[1]
    return pl.pallas_call(
        invert_kernel,
        out_shape=jax.ShapeDtypeStruct((columns // LANES, LANES), jnp.int32),
        in_specs=[HBM, ANY],
        out_specs=VMEM,
        scratch_shapes=[pltpu.VMEM(point_order.shape, jnp.int32), pltpu.SemaphoreType.DMA],
        compiler_params=params(),
        cost_estimate=took(1.0),
        name="invert",
    )(*in_hbm(point_order), after)


def near_kernel(first, tree_ref, inverse_hbm, after, near_ref, held, sems):
    chunks, _, width = held.shape
    copies = [
        pltpu.make_async_copy(
            inverse_hbm.at[:, pl.ds(first + i * width, width)], held.at[i], sems.at[i]
        )
        for i in range(chunks)
    ]
    for copy in copies:
        copy.start()
    for i, copy in enumerate(copies):
        copy.wait()
        near_ref[:, i * width : (i + 1) * width] = mm(tree_ref[...], held[i])


def near_strip(tree, leaf_inverse, strip, strips, after):
    rows, columns = tree.shape
    width = columns // strips
    chunk = 2 * LANES
    chunks = width // chunk
    return pl.pallas_call(
        functools.partial(near_kernel, strip * width),
        out_shape=jax.ShapeDtypeStruct((rows, width), F32),
        in_specs=[VMEM, HBM, ANY],
        out_specs=VMEM,
        scratch_shapes=[
            pltpu.VMEM((chunks, columns, chunk), BF),
            pltpu.SemaphoreType.DMA((chunks,)),
        ],
        compiler_params=params(),
        cost_estimate=took(5.6 / strips),
        name="near",
    )(tree, *in_hbm(leaf_inverse), after)


def join_kernel(mine, other, after, out_ref):
    rows = mine.shape[0]
    out_ref[:rows] = mine[...]
    out_ref[rows:] = other[...]


def join(mine, other, after):
    rows, rank = mine.shape
    return pl.pallas_call(
        join_kernel,
        out_shape=jax.ShapeDtypeStruct((2 * rows, rank), BF),
        in_specs=[VMEM] * 2 + [ANY],
        out_specs=VMEM,
        compiler_params=params(),
        cost_estimate=took(0.1),
        name="join",
    )(mine, other, after)


def leaf_kernel(pick, pair_own, pair_x, up_ref, after, g0_ref, out_ref):
    rows = out_ref.shape[0]
    table = [
        pair[m * rows : (m + 1) * rows, :].astype(F32) for pair in (pair_own, pair_x) for m in (0, 1)
    ]
    for m in range(SPREAD):
        g0_ref[m] = picked(pick[m : m + 1, :], table).astype(BF)
    out_ref[...] = mm(g0_ref[0], up_ref[...])


def leaf_rise(pick, pair_own, pair_x, leaf_up, after):
    double, rank = pair_own.shape
    rows = double // 2
    return pl.pallas_call(
        leaf_kernel,
        out_shape=(
            jax.ShapeDtypeStruct((SPREAD, rows, rank), BF),
            jax.ShapeDtypeStruct((rows, rank), F32),
        ),
        in_specs=[VMEM] * 4 + [ANY],
        out_specs=(VMEM,) * 2,
        compiler_params=params(),
        cost_estimate=took(0.4),
        name="leaf_rise",
    )(pick, pair_own, pair_x, leaf_up, after)


def node_kernel(mine, other, maps_own, maps_in, after, out_ref):
    rows, rank = mine.shape
    g1 = (mine[...] + other[...]).astype(BF)
    out_ref[:rows] = g1
    out_ref[rows:] = mm(g1, held(0, maps_own, maps_in, 0, rank)).astype(BF)


def node_rise(mine, other, maps, after):
    rows, rank = mine.shape
    return pl.pallas_call(
        node_kernel,
        out_shape=jax.ShapeDtypeStruct((2 * rows, rank), BF),
        in_specs=[VMEM] * 4 + [ANY],
        out_specs=VMEM,
        compiler_params=params(),
        cost_estimate=took(0.2),
        name="node_rise",
    )(mine, other, *maps, after)


def level_kernel(bit, mine, other, maps_own, maps_in, after, out_ref):
    rows = mine.shape[0] // 2
    rank = mine.shape[1]
    grown = (mine[rows:].astype(F32) + other[rows:].astype(F32)).astype(BF)
    out_ref[:rows] = grown
    out_ref[rows:] = mm(grown, held(bit, maps_own, maps_in, 0, rank)).astype(BF)


def level_rise(bit, mine, other, maps, after):
    double, rank = mine.shape
    return pl.pallas_call(
        functools.partial(level_kernel, bit),
        out_shape=jax.ShapeDtypeStruct((double, rank), BF),
        in_specs=[VMEM] * 4 + [ANY],
        out_specs=VMEM,
        compiler_params=params(),
        cost_estimate=took(0.25),
        name="level_rise",
    )(mine, other, *maps, after)


def fall_kernel(low_bit, count, *refs):
    mine, other = refs[:2]
    siblings = refs[2 : 1 + count]
    owns = refs[1 + count : 2 + 2 * count]
    arrivals = refs[2 + 2 * count : 3 + 3 * count]
    out = refs[4 + 3 * count]
    rows = mine.shape[0] // 2
    rank = mine.shape[1]
    top = (mine[rows:].astype(F32) + other[rows:].astype(F32)).astype(BF)

    def part(k, begin):
        return held(low_bit + min(k, 1), owns[k], arrivals[k], begin, rank)

    value = mm(top, part(count, 0)).astype(BF)
    for k in range(count, 0, -1):
        sibling = other[:rows] if k == count else siblings[k - 1][:rows]
        cross = part(k, owns[k].shape[0] - rank)
        value = (mm(sibling, cross) + mm(value, part(k - 1, rank))).astype(BF)
    out[...] = value


def fall(low_bit, mine, other, siblings, maps, after):
    count = len(maps) - 1
    double, rank = mine.shape
    return pl.pallas_call(
        functools.partial(fall_kernel, low_bit, count),
        out_shape=jax.ShapeDtypeStruct((double // 2, rank), BF),
        in_specs=[VMEM] * (3 + 3 * count) + [ANY],
        out_specs=VMEM,
        compiler_params=params(),
        cost_estimate=took(0.45),
        name="fall",
    )(mine, other, *siblings, *[m[0] for m in maps], *[m[1] for m in maps], after)


def step_kernel(bit, mine, other, sibling, maps_own, maps_in, block_own, block_in, after, out):
    rank = mine.shape[1]
    value = jnp.where(bit_of_device(bit), other[...], mine[...])
    cross = held(bit, maps_own, maps_in, 2 * rank, rank)
    down = held(bit - 1, block_own, block_in, rank, rank)
    out[...] = (mm(sibling[: mine.shape[0]], cross) + mm(value, down)).astype(BF)


def step_down(bit, mine, other, sibling, maps, block_maps, after):
    rows, rank = mine.shape
    return pl.pallas_call(
        functools.partial(step_kernel, bit),
        out_shape=jax.ShapeDtypeStruct((rows, rank), BF),
        in_specs=[VMEM] * 7 + [ANY],
        out_specs=VMEM,
        compiler_params=params(),
        cost_estimate=took(0.2),
        name="step_down",
    )(mine, other, sibling, *maps, *block_maps, after)


def local_kernel(g0_ref, node_pay, node_own, node_in, block_own, block_in, cross_in, down_ref, after, out_ref):
    rank = down_ref.shape[0]
    rows = node_pay.shape[0] // 2
    cross = held(1, block_own, block_in, 2 * rank, rank)
    cross = jnp.where(bit_of_device(0), cross_in[...], cross)
    inner = mm(node_pay[:rows], cross).astype(BF)
    out_ref[:rank] = mm(held(0, node_own, node_in, rank, rank), down_ref[...]).astype(BF)
    nearest = held(0, node_own, node_in, 2 * rank, rank)
    out_ref[rank:] = (mm(g0_ref[1], nearest) + mm(inner, down_ref[...])).astype(BF)


def local(g0, node_pay, node_maps, block_maps, block_cross, leaf_down, after):
    _, rows, rank = g0.shape
    return pl.pallas_call(
        local_kernel,
        out_shape=jax.ShapeDtypeStruct((rank + rows, rank), BF),
        in_specs=[VMEM] * 8 + [ANY],
        out_specs=VMEM,
        compiler_params=params(),
        cost_estimate=took(0.6),
        name="local",
    )(g0, node_pay, *node_maps, *block_maps, block_cross, leaf_down, after)


def choose_kernel(bit, upper, lower, after, out_ref):
    out_ref[...] = held(bit, upper, lower, 0, out_ref.shape[0])


def pass_kernel(block, after, out_ref):
    out_ref[...] = block[...]


def pass_on(block, after):
    return pl.pallas_call(
        pass_kernel,
        out_shape=jax.ShapeDtypeStruct(block.shape, block.dtype),
        in_specs=[VMEM, ANY],
        out_specs=VMEM,
        compiler_params=params(),
        cost_estimate=took(0.2),
        name="pass_on",
    )(block, after)


def choose(bit, upper, lower, after):
    return pl.pallas_call(
        functools.partial(choose_kernel, bit),
        out_shape=jax.ShapeDtypeStruct(upper.shape, BF),
        in_specs=[VMEM] * 2 + [ANY],
        out_specs=VMEM,
        compiler_params=params(),
        cost_estimate=took(0.2),
        name="choose",
    )(upper, lower, after)


def fold_kernel(strips, pick, l0, l1, l2, l3, out_basis, after, *refs):
    nears = refs[:strips]
    map_ref, base_ref = refs[strips:]
    rank = out_basis.shape[0]
    packs = (l0, l1, l2, l3)
    number = pick[SPREAD : SPREAD + 1, :]
    chosen = picked(number, [ref[:rank, :].astype(F32) for ref in packs]).astype(BF)
    inner = picked(number, [ref[rank:, :].astype(F32) for ref in packs]).astype(BF)
    map_ref[...] = mm(chosen, out_basis[...]).astype(BF)
    width = nears[0].shape[1]
    for i in range(strips):
        span = slice(i * width, (i + 1) * width)
        base_ref[:, span] = nears[i][...] + mm(inner, out_basis[:, span])


def fold(pick, locals_, basis_out, nears, after):
    rank, columns = basis_out.shape
    rows = nears[0].shape[0]
    return pl.pallas_call(
        functools.partial(fold_kernel, len(nears)),
        out_shape=(
            jax.ShapeDtypeStruct((rank, columns), BF),
            jax.ShapeDtypeStruct((rows, columns), F32),
        ),
        in_specs=[VMEM] * 6 + [ANY] + [VMEM] * len(nears),
        out_specs=(VMEM,) * 2,
        compiler_params=params(),
        cost_estimate=took(1.0),
        name="fold",
    )(pick, *locals_, basis_out, after, *nears)


def final_kernel(f_own, f_core, map_ref, base_ref, inv_ref, answer_hbm, total, answer, sems):
    f2 = jnp.where(bit_of_device(0), f_core[...], f_own[...])
    total[...] = base_ref[...] + mm(f2, map_ref[...])
    copies = []

    def store(tile, found):
        answer[:, tile * LANES : (tile + 1) * LANES] = found
        if tile % 4 == 3:
            span = pl.ds((tile - 3) * LANES, 4 * LANES)
            copies.append(
                pltpu.make_async_copy(
                    answer.at[:, span], answer_hbm.at[:, span], sems.at[len(copies)]
                )
            )
            copies[-1].start()

    gather_columns(total, lambda tile: inv_ref[tile : tile + 1, :], store)
    for copy in copies:
        copy.wait()


def final(f2, f2_core, leaf_map, base, inverse_order):
    rows, columns = base.shape
    return pl.pallas_call(
        final_kernel,
        out_shape=jax.ShapeDtypeStruct((rows, columns), F32),
        in_specs=[VMEM] * 5,
        out_specs=ANY,
        scratch_shapes=[
            pltpu.VMEM((rows, columns), F32),
            pltpu.VMEM((rows, columns), F32),
            pltpu.SemaphoreType.DMA((columns // (4 * LANES),)),
        ],
        compiler_params=params(),
        cost_estimate=took(1.8),
        name="final",
    )(f2, f2_core, leaf_map, base, inverse_order)


def body(
    right_sides,
    point_order,
    leaf_inverse,
    basis_in,
    basis_out,
    leaf_up,
    leaf_down,
    node_up,
    node_down,
    node_cross,
    leaf_map,
):
    members = lax.axis_size("leaf")
    levels = members.bit_length() - 1
    cut = SPREAD.bit_length() - 1
    me = lax.axis_index("leaf")
    rank = leaf_up.shape[1]
    offset = me & (SPREAD - 1)

    def cycle(bit):
        step = 1 << bit
        pairs = []
        for i in range(0, members, 2):
            if i & step == 0:
                pairs += [(i + step, i), (i, i | 1), (i | 1, (i + step) | 1), ((i + step) | 1, i + step)]
        return pairs

    def to_left(block, bit):
        if bit == 0:
            return swap(block, 1)
        return lax.ppermute(block, "leaf", cycle(bit))

    def to_right(block, bit):
        if bit == 0:
            return swap(block, 1)
        return lax.ppermute(block, "leaf", [(j, i) for i, j in cycle(bit)])

    pick, tree, reduced, low, high, top_low, top_high, up_map, down_map = start(
        right_sides, point_order, basis_in, leaf_map, leaf_up, leaf_down, node_up, node_down, node_cross
    )

    held_maps = {}

    def release(level, after):
        first, second = (top_low, top_high) if level == levels else (low, high)
        gate = pass_on(first, after)
        held_maps[level] = (second, to_left(gate, level - 1))
        return gate

    def spread(level, after):
        own, passed = held_maps[level]
        now = choose(level - 1, own, passed, after)
        for step in range(level - 2, cut, -1):
            passed = to_right(now, step)
            if step > cut + 1:
                now = choose(step, passed, now, after)
        held_maps[level] = (passed, now)

    pair = join(reduced, swap(reduced, 1), reduced)
    gate = release(cut, pair)
    node_maps = (high, swap(gate, 1))
    for level in [levels]:
        release(level, pair)
    g0, product = leaf_rise(pick, pair, swap(pair, 2), up_map, gate)
    gate = release(cut + 1, product)
    for level in range(cut + 2, levels):
        release(level, product)
    pay = node_rise(product, swap(product, 1), node_maps, gate)
    for level in []:
        release(level, pay)
    strips = 4
    nears = []
    arrivals = []
    for bit in range(1, levels - 1):
        arrivals.append(swap(pay, 1 << bit))
        after = pay
        if bit <= cut:
            after = near_strip(tree, leaf_inverse, len(nears), strips, pay)
            nears.append(after)
        if bit == cut:
            for level in range(cut + 3, levels + 1):
                spread(level, pay)
        if bit == cut + 1:
            pass
        pay = level_rise(min(bit, cut + 1), pay, arrivals[-1], held_maps[bit + 1], after)
        if bit == cut:
            own, passed = held_maps[cut]
            block_cross = choose(1, own[2 * rank :], passed[2 * rank :], pay)
            block_cross = to_right(block_cross, 0)

    own_local = local(g0, arrivals[0], node_maps, held_maps[cut], block_cross, down_map, pay)
    local_x = swap(own_local, 2)
    nears.append(near_strip(tree, leaf_inverse, 2, strips, pay))

    maps = [held_maps[level] for level in range(cut + 1, levels + 1)]
    cut_f = fall(cut, pay, swap(pay, 1 << (levels - 1)), arrivals[2:], maps, nears[2])
    nears.append(near_strip(tree, leaf_inverse, 3, strips, cut_f))
    block_f = step_down(
        cut, cut_f, swap(cut_f, SPREAD), arrivals[1], maps[0], held_maps[cut], nears[3]
    )
    inverse_order = invert(point_order, block_f)
    locals_ = [own_local, swap(own_local, 1), local_x, swap(pass_on(local_x, block_f), 1)]
    composed, base = fold(pick, locals_, basis_out, nears, inverse_order)
    block_f = choose(1, swap(block_f, 2), block_f, base)
    return final(block_f, swap(block_f, 1), composed, base, inverse_order)


def solution(mesh):
    placed = (
        P(None, "leaf"),
        P("leaf", None),
        P("leaf", None),
        P("leaf", None),
        P("leaf", None),
        P("leaf", None),
        P("leaf", None),
        P("leaf", None),
        P("leaf", None),
        P("leaf", None),
        P(),
    )
    return jax.shard_map(
        body, mesh=mesh, in_specs=placed, out_specs=P(None, "leaf"), check_vma=False
    )
```

```python
import functools

import jax
import jax.numpy as jnp
from jax import lax
from jax.experimental import pallas as pl
from jax.experimental.pallas import tpu as pltpu
from jax.sharding import PartitionSpec as P

SPREAD = 4
LANES = 128
BF = jnp.bfloat16
F32 = jnp.float32
VMEM = pl.BlockSpec(memory_space=pltpu.VMEM)
ANY = pl.BlockSpec(memory_space=pl.ANY)
HBM = pl.BlockSpec(memory_space=pltpu.HBM)
LIMIT = 32 * 2**20


def mm(a, b):
    return jnp.dot(a, b, preferred_element_type=F32)


def params():
    return pltpu.CompilerParams(vmem_limit_bytes=LIMIT)


def in_hbm(*arrays):
    return [pltpu.with_memory_space_constraint(array, pltpu.HBM) for array in arrays]


def took(micros):
    return pl.CostEstimate(flops=0, bytes_accessed=int(micros * 3e6), transcendentals=0)


def swap(block, mask):
    count = lax.axis_size("leaf")
    return lax.ppermute(block, "leaf", [(i, i ^ mask) for i in range(count)])


def bit_of_device(bit):
    return (lax.axis_index("leaf").astype(jnp.int32) & (1 << bit)) != 0


def picked(number, choices):
    number = number[:, :1]
    result = choices[0]
    for m in range(1, len(choices)):
        result = jnp.where(number == m, choices[m], result)
    return result


def held(bit, own, arrived, begin, size):
    rows = slice(begin, begin + size)
    if own is arrived:
        return own[rows, :]
    return jnp.where(bit_of_device(bit), own[rows, :], arrived[rows, :])


def gather_columns(table, slots, store):
    rows, columns = table.shape
    tiles = columns // LANES
    for out_tile in range(tiles):
        slot = jnp.broadcast_to(slots(out_tile), (rows, LANES))
        low = slot & (LANES - 1)
        high = slot // LANES
        found = None
        for tile in range(tiles):
            part = jnp.take_along_axis(
                table[:, tile * LANES : (tile + 1) * LANES], low, axis=1
            )
            found = part if found is None else jnp.where(high == tile, part, found)
        store(out_tile, found)


def start_kernel(rhs_hbm, order_hbm, basis_hbm, map_hbm, leaf_up, leaf_down, node_up, node_down, node_cross,
                 pick, tree_ref, red_ref, low_ref, high_ref, toplow_ref, tophigh_ref, up_ref, down_ref,
                 rhs, order, basis, table, seats, sems):
    rank = red_ref.shape[1]
    cross_low = node_cross.at[pl.ds(0, rank), :]
    cross_high = node_cross.at[pl.ds(rank, rank), :]
    copies = [
        pltpu.make_async_copy(rhs_hbm, rhs, sems.at[0]),
        pltpu.make_async_copy(order_hbm, order, sems.at[1]),
        pltpu.make_async_copy(map_hbm, seats, sems.at[2]),
        pltpu.make_async_copy(basis_hbm, basis, sems.at[3]),
    ]
    packs = (
        (low_ref, (node_up, node_down, cross_low)),
        (high_ref, (node_up, node_down, cross_high)),
        (toplow_ref, (node_up, cross_low)),
        (tophigh_ref, (node_up, cross_high)),
        (up_ref, (leaf_up,)),
        (down_ref, (leaf_down,)),
    )
    for dst, parts in packs:
        for i, part in enumerate(parts):
            copies.append(
                pltpu.make_async_copy(
                    part, dst.at[pl.ds(i * rank, rank), :], sems.at[len(copies)]
                )
            )
    for copy in copies:
        copy.start()
    copies[2].wait()
    me = lax.axis_index("leaf").astype(jnp.int32)
    offset = me & (SPREAD - 1)
    base = me - offset
    placed = [seats[base + slot] & (SPREAD - 1) for slot in range(SPREAD)]
    seat = placed[0]
    for slot in range(1, SPREAD):
        seat = jnp.where(offset == slot, placed[slot], seat)
    for m in range(SPREAD):
        source = jnp.int32(0)
        for slot in range(1, SPREAD):
            source = jnp.where(placed[slot] == (offset ^ m), slot, source)
        pick[m : m + 1, :] = jnp.full((1, LANES), source ^ offset, jnp.int32)
    pick[SPREAD : SPREAD + 1, :] = jnp.full((1, LANES), seat ^ offset, jnp.int32)
    copies[0].wait()
    table[...] = rhs[...].astype(F32)
    copies[1].wait()

    def store(tile, found):
        tree_ref[:, tile * LANES : (tile + 1) * LANES] = found.astype(BF)

    gather_columns(
        table, lambda tile: order[:, tile * LANES : (tile + 1) * LANES], store
    )
    copies[3].wait()
    red_ref[...] = mm(tree_ref[...], basis[...]).astype(BF)
    for copy in copies[4:]:
        copy.wait()


def start(right_sides, point_order, basis_in, leaf_map, *matrices):
    rows, columns = right_sides.shape
    rank = basis_in.shape[1]

    def block(count):
        return jax.ShapeDtypeStruct((count * rank, rank), BF)

    return pl.pallas_call(
        start_kernel,
        out_shape=(
            jax.ShapeDtypeStruct((2 * SPREAD, LANES), jnp.int32),
            jax.ShapeDtypeStruct((rows, columns), BF),
            jax.ShapeDtypeStruct((rows, rank), BF),
            block(3),
            block(3),
            block(2),
            block(2),
            block(1),
            block(1),
        ),
        in_specs=[HBM] * 9,
        out_specs=(VMEM,) * 9,
        scratch_shapes=[
            pltpu.VMEM(right_sides.shape, BF),
            pltpu.VMEM(point_order.shape, jnp.int32),
            pltpu.VMEM(basis_in.shape, BF),
            pltpu.VMEM(right_sides.shape, F32),
            pltpu.SMEM(leaf_map.shape, jnp.int32),
            pltpu.SemaphoreType.DMA((16,)),
        ],
        compiler_params=params(),
        cost_estimate=took(2.7),
        name="start",
    )(*in_hbm(right_sides, point_order, basis_in, leaf_map, *matrices))


def invert_kernel(order_hbm, after, inv_ref, order, sem):
    copy = pltpu.make_async_copy(order_hbm, order, sem)
    copy.start()
    copy.wait()
    slot = order[...]
    columns = slot.shape[1]
    tiles = columns // LANES
    low = slot & (LANES - 1)
    high = slot // LANES
    here = lax.broadcasted_iota(jnp.int32, (tiles, columns), 1)
    mask = lax.broadcasted_iota(jnp.int32, (tiles, columns), 0) == high
    left = jnp.concatenate(
        [
            jnp.where(mask, (here // LANES).astype(F32), 0.0),
            jnp.where(mask, (here & (LANES - 1)).astype(F32), 0.0),
        ],
        0,
    ).astype(BF)
    right = (lax.broadcasted_iota(jnp.int32, (LANES, columns), 0) == low).astype(F32).astype(BF)
    both = lax.dot_general(left, right, (((1,), (1,)), ((), ())), preferred_element_type=F32)
    inv_ref[...] = (both[:tiles] * LANES + both[tiles:]).astype(jnp.int32)


def invert(point_order, after):
    columns = point_order.shape[1]
    return pl.pallas_call(
        invert_kernel,
        out_shape=jax.ShapeDtypeStruct((columns // LANES, LANES), jnp.int32),
        in_specs=[HBM, ANY],
        out_specs=VMEM,
        scratch_shapes=[pltpu.VMEM(point_order.shape, jnp.int32), pltpu.SemaphoreType.DMA],
        compiler_params=params(),
        cost_estimate=took(1.0),
        name="invert",
    )(*in_hbm(point_order), after)


def near_kernel(first, tree_ref, inverse_hbm, after, near_ref, held, sems):
    chunks, _, width = held.shape
    copies = [
        pltpu.make_async_copy(
            inverse_hbm.at[:, pl.ds(first + i * width, width)], held.at[i], sems.at[i]
        )
        for i in range(chunks)
    ]
    for copy in copies:
        copy.start()
    for i, copy in enumerate(copies):
        copy.wait()
        near_ref[:, i * width : (i + 1) * width] = mm(tree_ref[...], held[i])


def near_strip(tree, leaf_inverse, strip, strips, after):
    rows, columns = tree.shape
    width = columns // strips
    chunk = 2 * LANES
    chunks = width // chunk
    return pl.pallas_call(
        functools.partial(near_kernel, strip * width),
        out_shape=jax.ShapeDtypeStruct((rows, width), F32),
        in_specs=[VMEM, HBM, ANY],
        out_specs=VMEM,
        scratch_shapes=[
            pltpu.VMEM((chunks, columns, chunk), BF),
            pltpu.SemaphoreType.DMA((chunks,)),
        ],
        compiler_params=params(),
        cost_estimate=took(5.6 / strips),
        name="near",
    )(tree, *in_hbm(leaf_inverse), after)


def join_kernel(mine, other, after, out_ref):
    rows = mine.shape[0]
    out_ref[:rows] = mine[...]
    out_ref[rows:] = other[...]


def join(mine, other, after):
    rows, rank = mine.shape
    return pl.pallas_call(
        join_kernel,
        out_shape=jax.ShapeDtypeStruct((2 * rows, rank), BF),
        in_specs=[VMEM] * 2 + [ANY],
        out_specs=VMEM,
        compiler_params=params(),
        cost_estimate=took(0.1),
        name="join",
    )(mine, other, after)


def leaf_kernel(pick, pair_own, pair_x, up_ref, after, g0_ref, out_ref):
    rows = out_ref.shape[0]
    table = [
        pair[m * rows : (m + 1) * rows, :].astype(F32) for pair in (pair_own, pair_x) for m in (0, 1)
    ]
    for m in range(SPREAD):
        g0_ref[m] = picked(pick[m : m + 1, :], table).astype(BF)
    out_ref[...] = mm(g0_ref[0], up_ref[...])


def leaf_rise(pick, pair_own, pair_x, leaf_up, after):
    double, rank = pair_own.shape
    rows = double // 2
    return pl.pallas_call(
        leaf_kernel,
        out_shape=(
            jax.ShapeDtypeStruct((SPREAD, rows, rank), BF),
            jax.ShapeDtypeStruct((rows, rank), F32),
        ),
        in_specs=[VMEM] * 4 + [ANY],
        out_specs=(VMEM,) * 2,
        compiler_params=params(),
        cost_estimate=took(0.4),
        name="leaf_rise",
    )(pick, pair_own, pair_x, leaf_up, after)


def node_kernel(mine, other, maps_own, maps_in, after, out_ref):
    rows, rank = mine.shape
    g1 = (mine[...] + other[...]).astype(BF)
    out_ref[:rows] = g1
    out_ref[rows:] = mm(g1, held(0, maps_own, maps_in, 0, rank)).astype(BF)


def node_rise(mine, other, maps, after):
    rows, rank = mine.shape
    return pl.pallas_call(
        node_kernel,
        out_shape=jax.ShapeDtypeStruct((2 * rows, rank), BF),
        in_specs=[VMEM] * 4 + [ANY],
        out_specs=VMEM,
        compiler_params=params(),
        cost_estimate=took(0.2),
        name="node_rise",
    )(mine, other, *maps, after)


def level_kernel(bit, mine, other, maps_own, maps_in, after, out_ref):
    rows = mine.shape[0] // 2
    rank = mine.shape[1]
    grown = (mine[rows:].astype(F32) + other[rows:].astype(F32)).astype(BF)
    out_ref[:rows] = grown
    out_ref[rows:] = mm(grown, held(bit, maps_own, maps_in, 0, rank)).astype(BF)


def level_rise(bit, mine, other, maps, after):
    double, rank = mine.shape
    return pl.pallas_call(
        functools.partial(level_kernel, bit),
        out_shape=jax.ShapeDtypeStruct((double, rank), BF),
        in_specs=[VMEM] * 4 + [ANY],
        out_specs=VMEM,
        compiler_params=params(),
        cost_estimate=took(0.25),
        name="level_rise",
    )(mine, other, *maps, after)


def fall_kernel(low_bit, count, *refs):
    mine, other = refs[:2]
    siblings = refs[2 : 1 + count]
    owns = refs[1 + count : 2 + 2 * count]
    arrivals = refs[2 + 2 * count : 3 + 3 * count]
    out = refs[4 + 3 * count]
    rows = mine.shape[0] // 2
    rank = mine.shape[1]
    top = (mine[rows:].astype(F32) + other[rows:].astype(F32)).astype(BF)

    def part(k, begin):
        return held(low_bit + min(k, 1), owns[k], arrivals[k], begin, rank)

    value = mm(top, part(count, 0)).astype(BF)
    for k in range(count, 0, -1):
        sibling = other[:rows] if k == count else siblings[k - 1][:rows]
        cross = part(k, owns[k].shape[0] - rank)
        value = (mm(sibling, cross) + mm(value, part(k - 1, rank))).astype(BF)
    out[...] = value


def fall(low_bit, mine, other, siblings, maps, after):
    count = len(maps) - 1
    double, rank = mine.shape
    return pl.pallas_call(
        functools.partial(fall_kernel, low_bit, count),
        out_shape=jax.ShapeDtypeStruct((double // 2, rank), BF),
        in_specs=[VMEM] * (3 + 3 * count) + [ANY],
        out_specs=VMEM,
        compiler_params=params(),
        cost_estimate=took(0.45),
        name="fall",
    )(mine, other, *siblings, *[m[0] for m in maps], *[m[1] for m in maps], after)


def step_kernel(bit, mine, other, sibling, maps_own, maps_in, block_own, block_in, after, out):
    rank = mine.shape[1]
    value = jnp.where(bit_of_device(bit), other[...], mine[...])
    cross = held(bit, maps_own, maps_in, 2 * rank, rank)
    down = held(bit - 1, block_own, block_in, rank, rank)
    out[...] = (mm(sibling[: mine.shape[0]], cross) + mm(value, down)).astype(BF)


def step_down(bit, mine, other, sibling, maps, block_maps, after):
    rows, rank = mine.shape
    return pl.pallas_call(
        functools.partial(step_kernel, bit),
        out_shape=jax.ShapeDtypeStruct((rows, rank), BF),
        in_specs=[VMEM] * 7 + [ANY],
        out_specs=VMEM,
        compiler_params=params(),
        cost_estimate=took(0.2),
        name="step_down",
    )(mine, other, sibling, *maps, *block_maps, after)


def local_kernel(g0_ref, node_pay, node_own, node_in, block_own, block_in, cross_in, down_ref, after, out_ref):
    rank = down_ref.shape[0]
    rows = node_pay.shape[0] // 2
    cross = held(1, block_own, block_in, 2 * rank, rank)
    cross = jnp.where(bit_of_device(0), cross_in[...], cross)
    inner = mm(node_pay[:rows], cross).astype(BF)
    out_ref[:rank] = mm(held(0, node_own, node_in, rank, rank), down_ref[...]).astype(BF)
    nearest = held(0, node_own, node_in, 2 * rank, rank)
    out_ref[rank:] = (mm(g0_ref[1], nearest) + mm(inner, down_ref[...])).astype(BF)


def local(g0, node_pay, node_maps, block_maps, block_cross, leaf_down, after):
    _, rows, rank = g0.shape
    return pl.pallas_call(
        local_kernel,
        out_shape=jax.ShapeDtypeStruct((rank + rows, rank), BF),
        in_specs=[VMEM] * 8 + [ANY],
        out_specs=VMEM,
        compiler_params=params(),
        cost_estimate=took(0.6),
        name="local",
    )(g0, node_pay, *node_maps, *block_maps, block_cross, leaf_down, after)


def choose_kernel(bit, upper, lower, after, out_ref):
    out_ref[...] = held(bit, upper, lower, 0, out_ref.shape[0])


def pass_kernel(block, after, out_ref):
    out_ref[...] = block[...]


def pass_on(block, after):
    return pl.pallas_call(
        pass_kernel,
        out_shape=jax.ShapeDtypeStruct(block.shape, block.dtype),
        in_specs=[VMEM, ANY],
        out_specs=VMEM,
        compiler_params=params(),
        cost_estimate=took(0.2),
        name="pass_on",
    )(block, after)


def choose(bit, upper, lower, after):
    return pl.pallas_call(
        functools.partial(choose_kernel, bit),
        out_shape=jax.ShapeDtypeStruct(upper.shape, BF),
        in_specs=[VMEM] * 2 + [ANY],
        out_specs=VMEM,
        compiler_params=params(),
        cost_estimate=took(0.2),
        name="choose",
    )(upper, lower, after)


def fold_kernel(strips, pick, l0, l1, l2, l3, out_basis, after, *refs):
    nears = refs[:strips]
    map_ref, base_ref = refs[strips:]
    rank = out_basis.shape[0]
    packs = (l0, l1, l2, l3)
    number = pick[SPREAD : SPREAD + 1, :]
    chosen = picked(number, [ref[:rank, :].astype(F32) for ref in packs]).astype(BF)
    inner = picked(number, [ref[rank:, :].astype(F32) for ref in packs]).astype(BF)
    map_ref[...] = mm(chosen, out_basis[...]).astype(BF)
    width = nears[0].shape[1]
    for i in range(strips):
        span = slice(i * width, (i + 1) * width)
        base_ref[:, span] = nears[i][...] + mm(inner, out_basis[:, span])


def fold(pick, locals_, basis_out, nears, after):
    rank, columns = basis_out.shape
    rows = nears[0].shape[0]
    return pl.pallas_call(
        functools.partial(fold_kernel, len(nears)),
        out_shape=(
            jax.ShapeDtypeStruct((rank, columns), BF),
            jax.ShapeDtypeStruct((rows, columns), F32),
        ),
        in_specs=[VMEM] * 6 + [ANY] + [VMEM] * len(nears),
        out_specs=(VMEM,) * 2,
        compiler_params=params(),
        cost_estimate=took(1.0),
        name="fold",
    )(pick, *locals_, basis_out, after, *nears)


def final_kernel(f_own, f_core, map_ref, base_ref, inv_ref, answer_hbm, total, answer, sems):
    f2 = jnp.where(bit_of_device(0), f_core[...], f_own[...])
    total[...] = base_ref[...] + mm(f2, map_ref[...])
    copies = []

    def store(tile, found):
        answer[:, tile * LANES : (tile + 1) * LANES] = found
        if tile % 4 == 3:
            span = pl.ds((tile - 3) * LANES, 4 * LANES)
            copies.append(
                pltpu.make_async_copy(
                    answer.at[:, span], answer_hbm.at[:, span], sems.at[len(copies)]
                )
            )
            copies[-1].start()

    gather_columns(total, lambda tile: inv_ref[tile : tile + 1, :], store)
    for copy in copies:
        copy.wait()


def final(f2, f2_core, leaf_map, base, inverse_order):
    rows, columns = base.shape
    return pl.pallas_call(
        final_kernel,
        out_shape=jax.ShapeDtypeStruct((rows, columns), F32),
        in_specs=[VMEM] * 5,
        out_specs=ANY,
        scratch_shapes=[
            pltpu.VMEM((rows, columns), F32),
            pltpu.VMEM((rows, columns), F32),
            pltpu.SemaphoreType.DMA((columns // (4 * LANES),)),
        ],
        compiler_params=params(),
        cost_estimate=took(1.8),
        name="final",
    )(f2, f2_core, leaf_map, base, inverse_order)


def body(
    right_sides,
    point_order,
    leaf_inverse,
    basis_in,
    basis_out,
    leaf_up,
    leaf_down,
    node_up,
    node_down,
    node_cross,
    leaf_map,
):
    members = lax.axis_size("leaf")
    levels = members.bit_length() - 1
    cut = SPREAD.bit_length() - 1
    me = lax.axis_index("leaf")
    rank = leaf_up.shape[1]
    offset = me & (SPREAD - 1)

    def cycle(bit):
        step = 1 << bit
        pairs = []
        for i in range(0, members, 2):
            if i & step == 0:
                pairs += [(i + step, i), (i, i | 1), (i | 1, (i + step) | 1), ((i + step) | 1, i + step)]
        return pairs

    def to_left(block, bit):
        if bit == 0:
            return swap(block, 1)
        return lax.ppermute(block, "leaf", cycle(bit))

    def to_right(block, bit):
        if bit == 0:
            return swap(block, 1)
        return lax.ppermute(block, "leaf", [(j, i) for i, j in cycle(bit)])

    pick, tree, reduced, low, high, top_low, top_high, up_map, down_map = start(
        right_sides, point_order, basis_in, leaf_map, leaf_up, leaf_down, node_up, node_down, node_cross
    )

    held_maps = {}

    def release(level, after):
        first, second = (top_low, top_high) if level == levels else (low, high)
        gate = pass_on(first, after)
        held_maps[level] = (second, to_left(gate, level - 1))
        return gate

    def spread(level, after):
        own, passed = held_maps[level]
        now = choose(level - 1, own, passed, after)
        for step in range(level - 2, cut, -1):
            passed = to_right(now, step)
            if step > cut + 1:
                now = choose(step, passed, now, after)
        held_maps[level] = (passed, now)

    pair = join(reduced, swap(reduced, 1), reduced)
    gate = release(cut, pair)
    node_maps = (high, swap(gate, 1))
    for level in [levels]:
        release(level, pair)
    g0, product = leaf_rise(pick, pair, swap(pair, 2), up_map, gate)
    gate = release(cut + 1, product)
    for level in range(cut + 2, levels):
        release(level, product)
    pay = node_rise(product, swap(product, 1), node_maps, gate)
    for level in []:
        release(level, pay)
    strips = 4
    nears = []
    arrivals = []
    for bit in range(1, levels - 1):
        arrivals.append(swap(pay, 1 << bit))
        after = pay
        if bit in (1, cut + 1):
            after = near_strip(tree, leaf_inverse, len(nears), strips, pay)
            nears.append(after)
        if bit == cut:
            for level in range(cut + 3, levels + 1):
                spread(level, pay)
        if bit == cut + 1:
            pass
        pay = level_rise(min(bit, cut + 1), pay, arrivals[-1], held_maps[bit + 1], after)
        if bit == cut:
            own, passed = held_maps[cut]
            block_cross = choose(1, own[2 * rank :], passed[2 * rank :], pay)
            block_cross = to_right(block_cross, 0)

    own_local = local(g0, arrivals[0], node_maps, held_maps[cut], block_cross, down_map, pay)
    local_x = swap(own_local, 2)
    nears.append(near_strip(tree, leaf_inverse, 2, strips, pay))

    maps = [held_maps[level] for level in range(cut + 1, levels + 1)]
    cut_f = fall(cut, pay, swap(pay, 1 << (levels - 1)), arrivals[2:], maps, nears[2])
    nears.append(near_strip(tree, leaf_inverse, 3, strips, cut_f))
    block_f = step_down(
        cut, cut_f, swap(cut_f, SPREAD), arrivals[1], maps[0], held_maps[cut], nears[3]
    )
    inverse_order = invert(point_order, block_f)
    locals_ = [own_local, swap(own_local, 1), local_x, swap(pass_on(local_x, block_f), 1)]
    composed, base = fold(pick, locals_, basis_out, nears, inverse_order)
    block_f = choose(1, swap(block_f, 2), block_f, base)
    return final(block_f, swap(block_f, 1), composed, base, inverse_order)


def solution(mesh):
    placed = (
        P(None, "leaf"),
        P("leaf", None),
        P("leaf", None),
        P("leaf", None),
        P("leaf", None),
        P("leaf", None),
        P("leaf", None),
        P("leaf", None),
        P("leaf", None),
        P("leaf", None),
        P(),
    )
    return jax.shard_map(
        body, mesh=mesh, in_specs=placed, out_specs=P(None, "leaf"), check_vma=False
    )
```

```python
import functools

import jax
import jax.numpy as jnp
from jax import lax
from jax.experimental import pallas as pl
from jax.experimental.pallas import tpu as pltpu
from jax.sharding import PartitionSpec as P

SPREAD = 4
LANES = 128
BF = jnp.bfloat16
F32 = jnp.float32
VMEM = pl.BlockSpec(memory_space=pltpu.VMEM)
ANY = pl.BlockSpec(memory_space=pl.ANY)
HBM = pl.BlockSpec(memory_space=pltpu.HBM)
LIMIT = 32 * 2**20


def mm(a, b):
    return jnp.dot(a, b, preferred_element_type=F32)


def params():
    return pltpu.CompilerParams(vmem_limit_bytes=LIMIT)


def in_hbm(*arrays):
    return [pltpu.with_memory_space_constraint(array, pltpu.HBM) for array in arrays]


def took(micros):
    return pl.CostEstimate(flops=0, bytes_accessed=int(micros * 3e6), transcendentals=0)


def swap(block, mask):
    count = lax.axis_size("leaf")
    return lax.ppermute(block, "leaf", [(i, i ^ mask) for i in range(count)])


def bit_of_device(bit):
    return (lax.axis_index("leaf").astype(jnp.int32) & (1 << bit)) != 0


def picked(number, choices):
    number = number[:, :1]
    result = choices[0]
    for m in range(1, len(choices)):
        result = jnp.where(number == m, choices[m], result)
    return result


def held(bit, own, arrived, begin, size):
    rows = slice(begin, begin + size)
    if own is arrived:
        return own[rows, :]
    return jnp.where(bit_of_device(bit), own[rows, :], arrived[rows, :])


def gather_columns(table, slots, store):
    rows, columns = table.shape
    tiles = columns // LANES
    for out_tile in range(tiles):
        slot = jnp.broadcast_to(slots(out_tile), (rows, LANES))
        low = slot & (LANES - 1)
        high = slot // LANES
        found = None
        for tile in range(tiles):
            part = jnp.take_along_axis(
                table[:, tile * LANES : (tile + 1) * LANES], low, axis=1
            )
            found = part if found is None else jnp.where(high == tile, part, found)
        store(out_tile, found)


def start_kernel(rhs_hbm, order_hbm, basis_hbm, map_hbm, leaf_up, leaf_down, node_up, node_down, node_cross,
                 pick, tree_ref, red_ref, low_ref, high_ref, toplow_ref, tophigh_ref, up_ref, down_ref,
                 rhs, order, basis, table, seats, sems):
    rank = red_ref.shape[1]
    cross_low = node_cross.at[pl.ds(0, rank), :]
    cross_high = node_cross.at[pl.ds(rank, rank), :]
    copies = [
        pltpu.make_async_copy(rhs_hbm, rhs, sems.at[0]),
        pltpu.make_async_copy(order_hbm, order, sems.at[1]),
        pltpu.make_async_copy(map_hbm, seats, sems.at[2]),
        pltpu.make_async_copy(basis_hbm, basis, sems.at[3]),
    ]
    packs = (
        (low_ref, (node_up, node_down, cross_low)),
        (high_ref, (node_up, node_down, cross_high)),
        (toplow_ref, (node_up, cross_low)),
        (tophigh_ref, (node_up, cross_high)),
        (up_ref, (leaf_up,)),
        (down_ref, (leaf_down,)),
    )
    for dst, parts in packs:
        for i, part in enumerate(parts):
            copies.append(
                pltpu.make_async_copy(
                    part, dst.at[pl.ds(i * rank, rank), :], sems.at[len(copies)]
                )
            )
    for copy in copies:
        copy.start()
    copies[2].wait()
    me = lax.axis_index("leaf").astype(jnp.int32)
    offset = me & (SPREAD - 1)
    base = me - offset
    placed = [seats[base + slot] & (SPREAD - 1) for slot in range(SPREAD)]
    seat = placed[0]
    for slot in range(1, SPREAD):
        seat = jnp.where(offset == slot, placed[slot], seat)
    for m in range(SPREAD):
        source = jnp.int32(0)
        for slot in range(1, SPREAD):
            source = jnp.where(placed[slot] == (offset ^ m), slot, source)
        pick[m : m + 1, :] = jnp.full((1, LANES), source ^ offset, jnp.int32)
    pick[SPREAD : SPREAD + 1, :] = jnp.full((1, LANES), seat ^ offset, jnp.int32)
    copies[0].wait()
    table[...] = rhs[...].astype(F32)
    copies[1].wait()

    def store(tile, found):
        tree_ref[:, tile * LANES : (tile + 1) * LANES] = found.astype(BF)

    gather_columns(
        table, lambda tile: order[:, tile * LANES : (tile + 1) * LANES], store
    )
    copies[3].wait()
    red_ref[...] = mm(tree_ref[...], basis[...]).astype(BF)
    for copy in copies[4:]:
        copy.wait()


def start(right_sides, point_order, basis_in, leaf_map, *matrices):
    rows, columns = right_sides.shape
    rank = basis_in.shape[1]

    def block(count):
        return jax.ShapeDtypeStruct((count * rank, rank), BF)

    return pl.pallas_call(
        start_kernel,
        out_shape=(
            jax.ShapeDtypeStruct((2 * SPREAD, LANES), jnp.int32),
            jax.ShapeDtypeStruct((rows, columns), BF),
            jax.ShapeDtypeStruct((rows, rank), BF),
            block(3),
            block(3),
            block(2),
            block(2),
            block(1),
            block(1),
        ),
        in_specs=[HBM] * 9,
        out_specs=(VMEM,) * 9,
        scratch_shapes=[
            pltpu.VMEM(right_sides.shape, BF),
            pltpu.VMEM(point_order.shape, jnp.int32),
            pltpu.VMEM(basis_in.shape, BF),
            pltpu.VMEM(right_sides.shape, F32),
            pltpu.SMEM(leaf_map.shape, jnp.int32),
            pltpu.SemaphoreType.DMA((16,)),
        ],
        compiler_params=params(),
        cost_estimate=took(2.7),
        name="start",
    )(*in_hbm(right_sides, point_order, basis_in, leaf_map, *matrices))


def invert_kernel(order_hbm, after, inv_ref, order, sem):
    copy = pltpu.make_async_copy(order_hbm, order, sem)
    copy.start()
    copy.wait()
    slot = order[...]
    columns = slot.shape[1]
    tiles = columns // LANES
    low = slot & (LANES - 1)
    high = slot // LANES
    here = lax.broadcasted_iota(jnp.int32, (tiles, columns), 1)
    mask = lax.broadcasted_iota(jnp.int32, (tiles, columns), 0) == high
    left = jnp.concatenate(
        [
            jnp.where(mask, (here // LANES).astype(F32), 0.0),
            jnp.where(mask, (here & (LANES - 1)).astype(F32), 0.0),
        ],
        0,
    ).astype(BF)
    right = (lax.broadcasted_iota(jnp.int32, (LANES, columns), 0) == low).astype(F32).astype(BF)
    both = lax.dot_general(left, right, (((1,), (1,)), ((), ())), preferred_element_type=F32)
    inv_ref[...] = (both[:tiles] * LANES + both[tiles:]).astype(jnp.int32)


def invert(point_order, after):
    columns = point_order.shape[1]
    return pl.pallas_call(
        invert_kernel,
        out_shape=jax.ShapeDtypeStruct((columns // LANES, LANES), jnp.int32),
        in_specs=[HBM, ANY],
        out_specs=VMEM,
        scratch_shapes=[pltpu.VMEM(point_order.shape, jnp.int32), pltpu.SemaphoreType.DMA],
        compiler_params=params(),
        cost_estimate=took(1.0),
        name="invert",
    )(*in_hbm(point_order), after)


def near_kernel(first, tree_ref, inverse_hbm, after, near_ref, held, sems):
    chunks, _, width = held.shape
    copies = [
        pltpu.make_async_copy(
            inverse_hbm.at[:, pl.ds(first + i * width, width)], held.at[i], sems.at[i]
        )
        for i in range(chunks)
    ]
    for copy in copies:
        copy.start()
    for i, copy in enumerate(copies):
        copy.wait()
        near_ref[:, i * width : (i + 1) * width] = mm(tree_ref[...], held[i])


def near_strip(tree, leaf_inverse, strip, strips, after):
    rows, columns = tree.shape
    width = columns // strips
    chunk = 2 * LANES
    chunks = width // chunk
    return pl.pallas_call(
        functools.partial(near_kernel, strip * width),
        out_shape=jax.ShapeDtypeStruct((rows, width), F32),
        in_specs=[VMEM, HBM, ANY],
        out_specs=VMEM,
        scratch_shapes=[
            pltpu.VMEM((chunks, columns, chunk), BF),
            pltpu.SemaphoreType.DMA((chunks,)),
        ],
        compiler_params=params(),
        cost_estimate=took(5.6 / strips),
        name="near",
    )(tree, *in_hbm(leaf_inverse), after)


def join_kernel(mine, other, after, out_ref):
    rows = mine.shape[0]
    out_ref[:rows] = mine[...]
    out_ref[rows:] = other[...]


def join(mine, other, after):
    rows, rank = mine.shape
    return pl.pallas_call(
        join_kernel,
        out_shape=jax.ShapeDtypeStruct((2 * rows, rank), BF),
        in_specs=[VMEM] * 2 + [ANY],
        out_specs=VMEM,
        compiler_params=params(),
        cost_estimate=took(0.1),
        name="join",
    )(mine, other, after)


def leaf_kernel(pick, pair_own, pair_x, up_ref, after, g0_ref, out_ref):
    rows = out_ref.shape[0]
    table = [
        pair[m * rows : (m + 1) * rows, :].astype(F32) for pair in (pair_own, pair_x) for m in (0, 1)
    ]
    for m in range(SPREAD):
        g0_ref[m] = picked(pick[m : m + 1, :], table).astype(BF)
    out_ref[...] = mm(g0_ref[0], up_ref[...])


def leaf_rise(pick, pair_own, pair_x, leaf_up, after):
    double, rank = pair_own.shape
    rows = double // 2
    return pl.pallas_call(
        leaf_kernel,
        out_shape=(
            jax.ShapeDtypeStruct((SPREAD, rows, rank), BF),
            jax.ShapeDtypeStruct((rows, rank), F32),
        ),
        in_specs=[VMEM] * 4 + [ANY],
        out_specs=(VMEM,) * 2,
        compiler_params=params(),
        cost_estimate=took(0.4),
        name="leaf_rise",
    )(pick, pair_own, pair_x, leaf_up, after)


def node_kernel(mine, other, maps_own, maps_in, after, out_ref):
    rows, rank = mine.shape
    g1 = (mine[...] + other[...]).astype(BF)
    out_ref[:rows] = g1
    out_ref[rows:] = mm(g1, held(0, maps_own, maps_in, 0, rank)).astype(BF)


def node_rise(mine, other, maps, after):
    rows, rank = mine.shape
    return pl.pallas_call(
        node_kernel,
        out_shape=jax.ShapeDtypeStruct((2 * rows, rank), BF),
        in_specs=[VMEM] * 4 + [ANY],
        out_specs=VMEM,
        compiler_params=params(),
        cost_estimate=took(0.2),
        name="node_rise",
    )(mine, other, *maps, after)


def level_kernel(bit, mine, other, maps_own, maps_in, after, out_ref):
    rows = mine.shape[0] // 2
    rank = mine.shape[1]
    grown = (mine[rows:].astype(F32) + other[rows:].astype(F32)).astype(BF)
    out_ref[:rows] = grown
    out_ref[rows:] = mm(grown, held(bit, maps_own, maps_in, 0, rank)).astype(BF)


def level_rise(bit, mine, other, maps, after):
    double, rank = mine.shape
    return pl.pallas_call(
        functools.partial(level_kernel, bit),
        out_shape=jax.ShapeDtypeStruct((double, rank), BF),
        in_specs=[VMEM] * 4 + [ANY],
        out_specs=VMEM,
        compiler_params=params(),
        cost_estimate=took(0.25),
        name="level_rise",
    )(mine, other, *maps, after)


def fall_kernel(low_bit, count, *refs):
    mine, other = refs[:2]
    siblings = refs[2 : 1 + count]
    owns = refs[1 + count : 2 + 2 * count]
    arrivals = refs[2 + 2 * count : 3 + 3 * count]
    out = refs[4 + 3 * count]
    rows = mine.shape[0] // 2
    rank = mine.shape[1]
    top = (mine[rows:].astype(F32) + other[rows:].astype(F32)).astype(BF)

    def part(k, begin):
        return held(low_bit + min(k, 1), owns[k], arrivals[k], begin, rank)

    value = mm(top, part(count, 0)).astype(BF)
    for k in range(count, 0, -1):
        sibling = other[:rows] if k == count else siblings[k - 1][:rows]
        cross = part(k, owns[k].shape[0] - rank)
        value = (mm(sibling, cross) + mm(value, part(k - 1, rank))).astype(BF)
    out[...] = value


def fall(low_bit, mine, other, siblings, maps, after):
    count = len(maps) - 1
    double, rank = mine.shape
    return pl.pallas_call(
        functools.partial(fall_kernel, low_bit, count),
        out_shape=jax.ShapeDtypeStruct((double // 2, rank), BF),
        in_specs=[VMEM] * (3 + 3 * count) + [ANY],
        out_specs=VMEM,
        compiler_params=params(),
        cost_estimate=took(0.45),
        name="fall",
    )(mine, other, *siblings, *[m[0] for m in maps], *[m[1] for m in maps], after)


def step_kernel(bit, mine, other, sibling, maps_own, maps_in, block_own, block_in, after, out):
    rank = mine.shape[1]
    value = jnp.where(bit_of_device(bit), other[...], mine[...])
    cross = held(bit, maps_own, maps_in, 2 * rank, rank)
    down = held(bit - 1, block_own, block_in, rank, rank)
    out[...] = (mm(sibling[: mine.shape[0]], cross) + mm(value, down)).astype(BF)


def step_down(bit, mine, other, sibling, maps, block_maps, after):
    rows, rank = mine.shape
    return pl.pallas_call(
        functools.partial(step_kernel, bit),
        out_shape=jax.ShapeDtypeStruct((rows, rank), BF),
        in_specs=[VMEM] * 7 + [ANY],
        out_specs=VMEM,
        compiler_params=params(),
        cost_estimate=took(0.2),
        name="step_down",
    )(mine, other, sibling, *maps, *block_maps, after)


def local_kernel(g0_ref, node_pay, node_own, node_in, block_own, block_in, cross_in, down_ref, after, out_ref):
    rank = down_ref.shape[0]
    rows = node_pay.shape[0] // 2
    cross = held(1, block_own, block_in, 2 * rank, rank)
    cross = jnp.where(bit_of_device(0), cross_in[...], cross)
    inner = mm(node_pay[:rows], cross).astype(BF)
    out_ref[:rank] = mm(held(0, node_own, node_in, rank, rank), down_ref[...]).astype(BF)
    nearest = held(0, node_own, node_in, 2 * rank, rank)
    out_ref[rank:] = (mm(g0_ref[1], nearest) + mm(inner, down_ref[...])).astype(BF)


def local(g0, node_pay, node_maps, block_maps, block_cross, leaf_down, after):
    _, rows, rank = g0.shape
    return pl.pallas_call(
        local_kernel,
        out_shape=jax.ShapeDtypeStruct((rank + rows, rank), BF),
        in_specs=[VMEM] * 8 + [ANY],
        out_specs=VMEM,
        compiler_params=params(),
        cost_estimate=took(0.6),
        name="local",
    )(g0, node_pay, *node_maps, *block_maps, block_cross, leaf_down, after)


def choose_kernel(bit, upper, lower, after, out_ref):
    out_ref[...] = held(bit, upper, lower, 0, out_ref.shape[0])


def pass_kernel(block, after, out_ref):
    out_ref[...] = block[...]


def pass_on(block, after):
    return pl.pallas_call(
        pass_kernel,
        out_shape=jax.ShapeDtypeStruct(block.shape, block.dtype),
        in_specs=[VMEM, ANY],
        out_specs=VMEM,
        compiler_params=params(),
        cost_estimate=took(0.2),
        name="pass_on",
    )(block, after)


def choose(bit, upper, lower, after):
    return pl.pallas_call(
        functools.partial(choose_kernel, bit),
        out_shape=jax.ShapeDtypeStruct(upper.shape, BF),
        in_specs=[VMEM] * 2 + [ANY],
        out_specs=VMEM,
        compiler_params=params(),
        cost_estimate=took(0.2),
        name="choose",
    )(upper, lower, after)


def fold_kernel(strips, pick, l0, l1, l2, l3, out_basis, after, *refs):
    nears = refs[:strips]
    map_ref, base_ref = refs[strips:]
    rank = out_basis.shape[0]
    packs = (l0, l1, l2, l3)
    number = pick[SPREAD : SPREAD + 1, :]
    chosen = picked(number, [ref[:rank, :].astype(F32) for ref in packs]).astype(BF)
    inner = picked(number, [ref[rank:, :].astype(F32) for ref in packs]).astype(BF)
    map_ref[...] = mm(chosen, out_basis[...]).astype(BF)
    width = nears[0].shape[1]
    for i in range(strips):
        span = slice(i * width, (i + 1) * width)
        base_ref[:, span] = nears[i][...] + mm(inner, out_basis[:, span])


def fold(pick, locals_, basis_out, nears, after):
    rank, columns = basis_out.shape
    rows = nears[0].shape[0]
    return pl.pallas_call(
        functools.partial(fold_kernel, len(nears)),
        out_shape=(
            jax.ShapeDtypeStruct((rank, columns), BF),
            jax.ShapeDtypeStruct((rows, columns), F32),
        ),
        in_specs=[VMEM] * 6 + [ANY] + [VMEM] * len(nears),
        out_specs=(VMEM,) * 2,
        compiler_params=params(),
        cost_estimate=took(1.0),
        name="fold",
    )(pick, *locals_, basis_out, after, *nears)


def final_kernel(f_own, f_core, f_x, f_both, map_ref, base_ref, inv_ref, answer_hbm, total, answer, sems):
    odd = bit_of_device(0)
    left = jnp.where(odd, f_core[...], f_own[...])
    right = jnp.where(odd, f_both[...], f_x[...])
    f2 = jnp.where(bit_of_device(1), right, left)
    total[...] = base_ref[...] + mm(f2, map_ref[...])
    copies = []

    def store(tile, found):
        answer[:, tile * LANES : (tile + 1) * LANES] = found
        if tile % 4 == 3:
            span = pl.ds((tile - 3) * LANES, 4 * LANES)
            copies.append(
                pltpu.make_async_copy(
                    answer.at[:, span], answer_hbm.at[:, span], sems.at[len(copies)]
                )
            )
            copies[-1].start()

    gather_columns(total, lambda tile: inv_ref[tile : tile + 1, :], store)
    for copy in copies:
        copy.wait()


def final(values, leaf_map, base, inverse_order):
    rows, columns = base.shape
    return pl.pallas_call(
        final_kernel,
        out_shape=jax.ShapeDtypeStruct((rows, columns), F32),
        in_specs=[VMEM] * 7,
        out_specs=ANY,
        scratch_shapes=[
            pltpu.VMEM((rows, columns), F32),
            pltpu.VMEM((rows, columns), F32),
            pltpu.SemaphoreType.DMA((columns // (4 * LANES),)),
        ],
        compiler_params=params(),
        cost_estimate=took(1.8),
        name="final",
    )(*values, leaf_map, base, inverse_order)


def body(
    right_sides,
    point_order,
    leaf_inverse,
    basis_in,
    basis_out,
    leaf_up,
    leaf_down,
    node_up,
    node_down,
    node_cross,
    leaf_map,
):
    members = lax.axis_size("leaf")
    levels = members.bit_length() - 1
    cut = SPREAD.bit_length() - 1
    me = lax.axis_index("leaf")
    rank = leaf_up.shape[1]
    offset = me & (SPREAD - 1)

    def cycle(bit):
        step = 1 << bit
        pairs = []
        for i in range(0, members, 2):
            if i & step == 0:
                pairs += [(i + step, i), (i, i | 1), (i | 1, (i + step) | 1), ((i + step) | 1, i + step)]
        return pairs

    def to_left(block, bit):
        if bit == 0:
            return swap(block, 1)
        return lax.ppermute(block, "leaf", cycle(bit))

    def to_right(block, bit):
        if bit == 0:
            return swap(block, 1)
        return lax.ppermute(block, "leaf", [(j, i) for i, j in cycle(bit)])

    pick, tree, reduced, low, high, top_low, top_high, up_map, down_map = start(
        right_sides, point_order, basis_in, leaf_map, leaf_up, leaf_down, node_up, node_down, node_cross
    )

    held_maps = {}

    def release(level, after):
        first, second = (top_low, top_high) if level == levels else (low, high)
        gate = pass_on(first, after)
        held_maps[level] = (second, to_left(gate, level - 1))
        return gate

    def spread(level, after):
        own, passed = held_maps[level]
        now = choose(level - 1, own, passed, after)
        for step in range(level - 2, cut, -1):
            passed = to_right(now, step)
            if step > cut + 1:
                now = choose(step, passed, now, after)
        held_maps[level] = (passed, now)

    pair = join(reduced, swap(reduced, 1), reduced)
    gate = release(cut, pair)
    node_maps = (high, swap(gate, 1))
    for level in [levels]:
        release(level, pair)
    g0, product = leaf_rise(pick, pair, swap(pair, 2), up_map, gate)
    gate = release(cut + 1, product)
    for level in range(cut + 2, levels):
        release(level, product)
    pay = node_rise(product, swap(product, 1), node_maps, gate)
    for level in []:
        release(level, pay)
    strips = 4
    nears = []
    arrivals = []
    for bit in range(1, levels - 1):
        arrivals.append(swap(pay, 1 << bit))
        after = pay
        if bit in (1, cut + 1):
            after = near_strip(tree, leaf_inverse, len(nears), strips, pay)
            nears.append(after)
        if bit == cut:
            for level in range(cut + 3, levels + 1):
                spread(level, pay)
        if bit == cut + 1:
            pass
        pay = level_rise(min(bit, cut + 1), pay, arrivals[-1], held_maps[bit + 1], after)
        if bit == cut:
            own, passed = held_maps[cut]
            block_cross = choose(1, own[2 * rank :], passed[2 * rank :], pay)
            block_cross = to_right(block_cross, 0)

    own_local = local(g0, arrivals[0], node_maps, held_maps[cut], block_cross, down_map, pay)
    local_x = swap(own_local, 2)
    nears.append(near_strip(tree, leaf_inverse, 2, strips, pay))

    maps = [held_maps[level] for level in range(cut + 1, levels + 1)]
    cut_f = fall(cut, pay, swap(pay, 1 << (levels - 1)), arrivals[2:], maps, nears[2])
    nears.append(near_strip(tree, leaf_inverse, 3, strips, cut_f))
    block_f = step_down(
        cut, cut_f, swap(cut_f, SPREAD), arrivals[1], maps[0], held_maps[cut], nears[3]
    )
    inverse_order = invert(point_order, block_f)
    locals_ = [own_local, swap(own_local, 1), local_x, swap(pass_on(local_x, block_f), 1)]
    composed, base = fold(pick, locals_, basis_out, nears, inverse_order)
    values = [block_f] + [swap(block_f, m) for m in range(1, SPREAD)]
    return final(values, composed, base, inverse_order)


def solution(mesh):
    placed = (
        P(None, "leaf"),
        P("leaf", None),
        P("leaf", None),
        P("leaf", None),
        P("leaf", None),
        P("leaf", None),
        P("leaf", None),
        P("leaf", None),
        P("leaf", None),
        P("leaf", None),
        P(),
    )
    return jax.shard_map(
        body, mesh=mesh, in_specs=placed, out_specs=P(None, "leaf"), check_vma=False
    )
```
